768 devices in a mesh: tile: 192 (over z, y_lo, x, core), mode: 4 (over y_hi).
Axes of the slice: x: 4, y: 8 (y_hi: 4, y_lo: 2; y = y_hi * 2 + y_lo), z: 12, core: 2. Of those that a mesh axis runs over, the one named last changes fastest.
Arguments:
- object_field: float32 [2, 24576, 1024], P(None, 'tile'), may hold values from -5 to 5
- components: float32 [4, 4, 2, 128, 128], P('mode'), may hold values from -4 to 4
- relax_weights: float32 [1536, 4], P('tile'), may hold values from -4 to 4
- amplitudes: float32 [1536, 128, 128], P('tile'), may hold values from 0.2 to 4
- positions: int32 [1536, 2], P('tile'), may hold values from 0 to 24575, as said below
- counts: int32 [192], P('tile'), may hold values from 1 to 8, as said below
Outputs:
- object_grad: float32 [2, 24576, 1024], P(None, 'tile', 'mode')
- probe_grad: float32 [4, 4, 2, 128, 128], P('mode')
The draws below stay inside these ranges and needn't reach their ends.
Inputs may be any that keep to these rules, and one draw needn't show every extreme that they name: positions[j, 0] lies in the rows of the band that holds slot j (128 rows from band index times 128); positions[j, 1] is at most 896; every band has a slot at its last row and one at the last column. `counts`: some band uses all its slots.
All inputs are finite; a program needn't handle non-finite values.
Results may differ from the reference program's by a relative error of at most 0.0003.
Values sent between devices are 32-bit elements; how exact they have to be, the bound alone decides.
A program may use at most 32 MiB of HBM per device.

```python
import math
import jax
import jax.numpy as jnp
from jax import lax

P_SIZE = 128
COMP = 4
TH = 128
OW = 1024
SLOTS = 8
MODES = 4
TILES = 192
ROWS = 24576
POSITIONS = 1536


def draw_positions(key, part):
    key_row, key_col, key_pick_row, key_pick_col = jax.random.split(key, 4)
    every = jnp.arange(TILES * SLOTS, dtype=jnp.int32)
    band_index = every // SLOTS
    slot_index = every % SLOTS
    local_row = jax.random.randint(key_row, (TILES * SLOTS,), 0, TH, dtype=jnp.int32)
    column = jax.random.randint(key_col, (TILES * SLOTS,), 0, OW - P_SIZE + 1, dtype=jnp.int32)
    pick_row = jax.random.randint(key_pick_row, (TILES,), 0, SLOTS, dtype=jnp.int32)
    pick_col = jax.random.randint(key_pick_col, (TILES,), 0, SLOTS, dtype=jnp.int32)
    local_row = jnp.where(slot_index == pick_row[band_index], TH - 1, local_row)
    column = jnp.where(slot_index == pick_col[band_index], OW - P_SIZE, column)
    return jnp.stack([band_index * TH + local_row, column], axis=1)


def draw_counts(key, part):
    key_count, key_full = jax.random.split(jax.random.fold_in(key, 7), 2)
    lowest = max(SLOTS // 4, 1)
    used = jax.random.randint(key_count, (TILES,), lowest, SLOTS + 1, dtype=jnp.int32)
    full_band = jax.random.randint(key_full, (), 0, TILES, dtype=jnp.int32)
    return jnp.where(jnp.arange(TILES, dtype=jnp.int32) == full_band, SLOTS, used)


def block_scale(stream_key, extent, cuts, least, high):
    gain = 1.0
    for axis_at, shards_of in cuts:
        steps = jax.random.uniform(jax.random.fold_in(jax.random.fold_in(stream_key, 6), axis_at), (shards_of,), jnp.float32, least / len(cuts), high / len(cuts))
        gain = gain * jnp.repeat(jnp.exp(steps), extent[axis_at] // shards_of).reshape((-1,) + (1,) * (len(extent) - 1 - axis_at))
    return gain


def bell_draw(rng, shape, spread, most, cuts=(), kind=jnp.bfloat16):
    gain = block_scale(rng, shape, cuts, -0.22, 0.18) if cuts else 1.0
    array = jax.random.normal(rng, shape, jnp.float32) * spread * gain
    return jnp.minimum(jnp.maximum(array, -most), most).astype(kind)


def setup_inputs(seed: int = 0) -> dict:
    arg_keys = jax.random.split(jax.random.key(seed), 7)
    object_field = bell_draw(arg_keys[0], (2, ROWS, OW), 0.7, 5.0, ((1, 192),), jnp.float32)
    components = bell_draw(arg_keys[1], (MODES, COMP, 2, P_SIZE, P_SIZE), 0.5, 4.0, ((0, 4),), jnp.float32)
    relax_weights = bell_draw(arg_keys[2], (POSITIONS, COMP), 1.0, 4.0, ((0, 192),), jnp.float32)
    amplitudes = jnp.clip(jnp.exp(math.log(4.0) - 2.9957323 * jax.random.uniform(arg_keys[3], (POSITIONS, P_SIZE, P_SIZE), jnp.float32) ** block_scale(arg_keys[3], (POSITIONS, P_SIZE, P_SIZE), ((0, 192),), -0.2, 0.2)), 0.2, 4.0)
    positions = draw_positions(jax.random.fold_in(arg_keys[6], 71), 0)
    counts = draw_counts(jax.random.fold_in(arg_keys[6], 71), 0)
    return {"object_field": object_field, "components": components, "relax_weights": relax_weights, "amplitudes": amplitudes, "positions": positions, "counts": counts}


def make_tables(patch_size):
    index_line = jnp.arange(patch_size, dtype=jnp.int32)
    product = index_line[:, None] * index_line[None, :] % patch_size
    angle = product.astype(jnp.float32) * (2.0 * math.pi / patch_size)
    scale = 1.0 / math.sqrt(patch_size)
    return (jnp.cos(angle) * scale, -jnp.sin(angle) * scale)

def complex_product(left_part, right_part):
    left_re = left_part[..., 0, :, :]
    left_im = left_part[..., 1, :, :]
    right_re = right_part[..., 0, :, :]
    right_im = right_part[..., 1, :, :]
    return jnp.stack([left_re * right_re - left_im * right_im, left_re * right_im + left_im * right_re], axis=-3)

def conjugate(field):
    return jnp.stack([field[..., 0, :, :], -field[..., 1, :, :]], axis=-3)

def transform(field, cos_table, sin_table):
    highest = lax.Precision.HIGHEST
    real_part = field[..., 0, :, :]
    imag_part = field[..., 1, :, :]

    def on_left(matrix, values):
        return jnp.einsum('ab,...bc->...ac', matrix, values, precision=highest)

    def on_right(values, matrix):
        return jnp.einsum('...ab,bc->...ac', values, matrix, precision=highest)
    middle_re = on_left(cos_table, real_part) - on_left(sin_table, imag_part)
    middle_im = on_left(cos_table, imag_part) + on_left(sin_table, real_part)
    out_re = on_right(middle_re, cos_table) - on_right(middle_im, sin_table)
    out_im = on_right(middle_re, sin_table) + on_right(middle_im, cos_table)
    return jnp.stack([out_re, out_im], axis=-3)

def reference(object_field, components, relax_weights, amplitudes, positions, counts):
    highest = lax.Precision.HIGHEST
    cos_table, sin_table = make_tables(P_SIZE)
    padded = jnp.pad(object_field, ((0, 0), (0, P_SIZE), (0, 0)))
    slot_index = jnp.arange(POSITIONS, dtype=jnp.int32) % SLOTS
    band_index = jnp.arange(POSITIONS, dtype=jnp.int32) // SLOTS
    alive_mask = (slot_index < counts[band_index]).astype(jnp.float32)
    zero_index = jnp.zeros((), jnp.int32)

    def advance(carry, item):
        grad_field, grad_probe = carry
        place, weight_row, measured, alive = item
        row_at = place[0].astype(jnp.int32)
        col_at = place[1].astype(jnp.int32)
        patch = lax.dynamic_slice(padded, (zero_index, row_at, col_at), (2, P_SIZE, P_SIZE))
        probes = jnp.einsum('c,kcxyz->kxyz', weight_row, components, precision=highest)
        far_field = transform(complex_product(probes, patch[None]), cos_table, sin_table)
        intensity = lax.optimization_barrier(jnp.sum(far_field * far_field, axis=(0, 1)))
        factor = alive * (1.0 - measured / jnp.sqrt(jnp.maximum(intensity, 1.0)))
        residue = far_field * factor
        back_waves = transform(residue, cos_table, -sin_table)
        patch_grad = lax.optimization_barrier(jnp.sum(complex_product(conjugate(probes), back_waves), axis=0))
        current = lax.dynamic_slice(grad_field, (zero_index, row_at, col_at), (2, P_SIZE, P_SIZE))
        grad_field = lax.dynamic_update_slice(grad_field, current + patch_grad, (zero_index, row_at, col_at))
        probe_terms = complex_product(conjugate(patch)[None], back_waves)
        grad_probe = grad_probe + weight_row[None, :, None, None, None] * probe_terms[:, None]
        return ((grad_field, grad_probe), None)
    start = (jnp.zeros_like(padded), jnp.zeros_like(components))
    (grad_field, grad_probe), unused = lax.scan(advance, start, (positions, relax_weights, amplitudes, alive_mask))
    return (grad_field[:, :ROWS, :], grad_probe)
```

```python
import functools
import math

import jax
import jax.numpy as jnp
import numpy as np
from jax import lax
from jax.experimental import pallas as pl
from jax.experimental.pallas import tpu as pltpu
from jax.sharding import PartitionSpec as P

MESH = pl.DeviceIdType.MESH
SIDE = 128
SLOTS = 8
COMP = 4
MODES = 4
TILES_WIDE = 8
QUARTER = 32
HALF = 16
EMPTY = 2 * SLOTS


def group_size(tiles):
    return 16 if tiles % 16 == 0 else 2


def owner_count(depth):
    return 1 << (depth.bit_length() - 1)


def split(values):
    high = values.astype(jnp.bfloat16)
    low = (values - high.astype(jnp.float32)).astype(jnp.bfloat16)
    return high, low


def dot(left, right):
    return jnp.dot(left, right, preferred_element_type=jnp.float32)


def both_sides(wide, right_high, right_low, left_high, left_low):
    high, low = split(wide)
    middle = dot(high, right_high) + dot(low, right_high) + dot(high, right_low)
    tall = jnp.concatenate([middle[:, :SIDE], middle[:, SIDE:]], axis=0)
    high, low = split(tall)
    return dot(left_high, high) + dot(left_high, low) + dot(left_low, high)


def kernel(
    tiles,
    object_ref,
    components_ref,
    weights_ref,
    amplitudes_ref,
    positions_ref,
    counts_ref,
    row_high,
    row_low,
    col_high,
    col_low,
    object_out,
    probe_out,
    ext,
    comp,
    amps,
    patches,
    probes,
    far,
    power,
    pair_in,
    pair_mid,
    pair_sum,
    factor,
    placed,
    rim_out,
    rim_in,
    part,
    part_in,
    terms,
    chunk,
    near_buf,
    far_buf,
    local_sems,
    halo_sems,
    slot_sems,
    rim_sems,
    part_sems,
    near_sems,
    far_sems,
    back_sems,
    spread_sems,
):
    group = group_size(tiles)
    depth = tiles // group
    owners = owner_count(depth)
    rows = COMP * 2 * SIDE // group
    piece = rows // owners
    tile = lax.axis_index("tile")
    mode = lax.axis_index("mode")
    above = lax.rem(tile + tiles - 1, tiles)
    below = lax.rem(tile + 1, tiles)
    right = lax.rem(mode + 1, MODES)
    left = lax.rem(mode + MODES - 1, MODES)
    mine = lax.rem(tile, group)
    level = lax.div(tile, group)

    def near(step):
        return level * group + lax.rem(mine + step, group)

    def beyond(step):
        return lax.rem(level + step, depth) * group + mine

    def send(src, dst, sems, peer):
        return pltpu.make_async_remote_copy(
            src_ref=src,
            dst_ref=dst,
            send_sem=sems.at[0],
            recv_sem=sems.at[1],
            device_id=peer,
            device_id_type=MESH,
        )

    def columns(ref, at):
        return ref.at[:, :, pl.ds(at * SIDE, SIDE)]

    loads = [
        pltpu.make_async_copy(components_ref.at[0], comp, local_sems.at[0]),
        pltpu.make_async_copy(
            amplitudes_ref.at[:, pl.ds(pl.multiple_of(mode * QUARTER, 8), QUARTER), :],
            amps,
            local_sems.at[1],
        ),
    ] + [
        pltpu.make_async_copy(
            columns(object_ref, at), ext.at[:, at, pl.ds(0, SIDE), :], local_sems.at[2 + at]
        )
        for at in range(TILES_WIDE)
    ]
    for copy in loads:
        copy.start()

    barrier = pltpu.get_barrier_semaphore()
    peers = [{"tile": above}, {"tile": below}, {"mode": right}, {"mode": left}]
    peers += [{"tile": near(step)} for step in range(1, group)]
    peers += [{"tile": beyond(step)} for step in range(1, depth)]
    for peer in peers:
        pl.semaphore_signal(barrier, inc=1, device_id=peer, device_id_type=MESH)
    pl.semaphore_wait(barrier, len(peers))

    halo = [
        send(
            columns(object_ref, at),
            ext.at[:, at, pl.ds(SIDE, SIDE), :],
            halo_sems.at[:, at],
            {"tile": above},
        )
        for at in range(TILES_WIDE)
    ]
    for copy in halo:
        copy.start()

    terms[...] = jnp.zeros_like(terms)

    def clear(at, carry):
        for plane in range(2):
            placed[plane, at, pl.ds(0, SIDE), :] = jnp.zeros((SIDE, SIDE), jnp.float32)
            placed[plane, at, pl.ds(2 * SIDE, SIDE), :] = jnp.zeros((SIDE, SIDE), jnp.float32)
        return carry

    lax.fori_loop(0, EMPTY + 1, clear, 0)
    for plane in range(2):
        placed[plane, EMPTY, pl.ds(SIDE, SIDE), :] = jnp.zeros((SIDE, SIDE), jnp.float32)
    for copy in loads:
        copy.wait()

    def mix(slot, carry):
        for plane in range(2):
            total = weights_ref[slot, 0] * comp[0, plane]
            for at in range(1, COMP):
                total = total + weights_ref[slot, at] * comp[at, plane]
            probes[slot, plane] = total
        return carry

    lax.fori_loop(0, SLOTS, mix, 0)
    for copy in halo:
        copy.wait_recv()

    @pl.when(tile == tiles - 1)
    def _():
        for plane in range(2):
            for at in range(TILES_WIDE):
                ext[plane, at, pl.ds(SIDE, SIDE), :] = jnp.zeros((SIDE, SIDE), jnp.float32)

    lane = lax.broadcasted_iota(jnp.int32, (SIDE, SIDE), 1)

    def place_of(slot):
        row = positions_ref[slot, 0] & (SIDE - 1)
        col = positions_ref[slot, 1]
        base = jnp.minimum(lax.shift_right_logical(col, 7), TILES_WIDE - 2)
        return row, base, col - base * SIDE

    def take(slot, plane):
        row, base, shift = place_of(slot)
        turn = (SIDE - shift) & (SIDE - 1)
        first = pltpu.roll(ext[plane, base, pl.ds(row, SIDE), :], turn, 1)
        second = pltpu.roll(ext[plane, base + 1, pl.ds(row, SIDE), :], turn, 1)
        return jnp.where(lane < SIDE - shift, first, second)

    ahead = pl.multiple_of(lax.rem(QUARTER * (mode + 1) + HALF, SIDE), 8)
    behind = pl.multiple_of(lax.rem(QUARTER * (mode + 2) + HALF, SIDE), 8)
    own_rows = pl.multiple_of(QUARTER * mode, 8)
    right_rows = pl.multiple_of(QUARTER * right, 8)
    left_rows = pl.multiple_of(QUARTER * left, 8)

    def first_pass(slot):
        return [
            send(
                power.at[slot, pl.ds(ahead, QUARTER), :],
                pair_in.at[slot, 0],
                slot_sems.at[:, slot, 0],
                {"mode": right},
            ),
            send(
                power.at[slot, pl.ds(behind, QUARTER), :],
                pair_in.at[slot, 1],
                slot_sems.at[:, slot, 1],
                {"mode": left},
            ),
        ]

    def second_pass(slot):
        return [
            send(
                pair_mid.at[slot, 0],
                pair_sum.at[slot, 0],
                slot_sems.at[:, slot, 2],
                {"mode": right},
            ),
            send(
                pair_mid.at[slot, 1],
                pair_sum.at[slot, 1],
                slot_sems.at[:, slot, 3],
                {"mode": left},
            ),
        ]

    def factor_rows(slot, start, count):
        return factor.at[slot, pl.ds(start, count), :]

    def third_pass(slot):
        mid = factor_rows(slot, own_rows, QUARTER)
        return [
            send(mid, mid, slot_sems.at[:, slot, 4], {"mode": right}),
            send(mid, mid, slot_sems.at[:, slot, 5], {"mode": left}),
        ]

    def fourth_pass(slot):
        top = factor_rows(slot, left_rows, HALF)
        bottom = factor_rows(slot, pl.multiple_of(right_rows + HALF, 8), HALF)
        return [
            send(top, top, slot_sems.at[:, slot, 6], {"mode": right}),
            send(bottom, bottom, slot_sems.at[:, slot, 7], {"mode": left}),
        ]

    def forward(slot):
        for plane in range(2):
            patches[slot, plane] = take(slot, plane)
        probe_re, probe_im = probes[slot, 0], probes[slot, 1]
        patch_re, patch_im = patches[slot, 0], patches[slot, 1]
        wide = jnp.concatenate(
            [
                probe_re * patch_re - probe_im * patch_im,
                probe_re * patch_im + probe_im * patch_re,
            ],
            axis=1,
        )
        wave = both_sides(wide, row_high[...], row_low[...], col_high[...], col_low[...])
        far[slot] = wave
        strength = wave[:SIDE] * wave[:SIDE] + wave[SIDE:] * wave[SIDE:]
        power[slot, pl.ds(0, SIDE), :] = strength
        power[slot, pl.ds(SIDE, HALF), :] = strength[:HALF]
        for copy in first_pass(slot):
            copy.start()

    def relay_power(slot):
        to_right, to_left = first_pass(slot)
        go_right, go_left = second_pass(slot)
        to_right.wait_recv()
        pair_mid[slot, 0] = pair_in[slot, 0, pl.ds(HALF, HALF), :] + power[slot, pl.ds(right_rows, HALF), :]
        go_right.start()
        to_left.wait_recv()
        pair_mid[slot, 1] = (
            pair_in[slot, 1, pl.ds(0, HALF), :]
            + power[slot, pl.ds(pl.multiple_of(left_rows + HALF, 8), HALF), :]
        )
        go_left.start()

    def make_factor(slot):
        for copy in second_pass(slot):
            copy.wait_recv()
        own = power[slot, pl.ds(own_rows, QUARTER), :]
        top = own[:HALF] + pair_sum[slot, 0] + pair_in[slot, 1, pl.ds(HALF, HALF), :]
        bottom = own[HALF:] + pair_sum[slot, 1] + pair_in[slot, 0, pl.ds(0, HALF), :]
        intensity = jnp.concatenate([top, bottom], axis=0)
        ratio = 1.0 - amps[slot] * lax.rsqrt(jnp.maximum(intensity, 1.0))
        factor[slot, pl.ds(own_rows, QUARTER), :] = jnp.where(slot < counts_ref[0], ratio, 0.0)
        for copy in third_pass(slot):
            copy.start()

    def relay_factor(slot):
        go_right, go_left = fourth_pass(slot)
        from_left = factor_rows(slot, left_rows, QUARTER)
        send(from_left, from_left, slot_sems.at[:, slot, 4], {"mode": right}).wait_recv()
        go_right.start()
        from_right = factor_rows(slot, right_rows, QUARTER)
        send(from_right, from_right, slot_sems.at[:, slot, 5], {"mode": left}).wait_recv()
        go_left.start()

    def backward(slot):
        across = pl.multiple_of(QUARTER * lax.rem(mode + 2, MODES), 8)
        top = factor_rows(slot, across, HALF)
        send(top, top, slot_sems.at[:, slot, 6], {"mode": right}).wait_recv()
        bottom = factor_rows(slot, pl.multiple_of(across + HALF, 8), HALF)
        send(bottom, bottom, slot_sems.at[:, slot, 7], {"mode": left}).wait_recv()
        scale = factor[slot]
        wave = far[slot]
        wide = jnp.concatenate([wave[:SIDE] * scale, wave[SIDE:] * scale], axis=1)
        back = both_sides(wide, col_high[...], col_low[...], row_high[...], row_low[...])
        back_re, back_im = back[:SIDE], back[SIDE:]
        probe_re, probe_im = probes[slot, 0], probes[slot, 1]
        shift = place_of(slot)[2]
        grads = (
            probe_re * back_re + probe_im * back_im,
            probe_re * back_im - probe_im * back_re,
        )
        for plane in range(2):
            turned = pltpu.roll(grads[plane], shift & (SIDE - 1), 1)
            placed[plane, 2 * slot, pl.ds(SIDE, SIDE), :] = jnp.where(lane >= shift, turned, 0.0)
            placed[plane, 2 * slot + 1, pl.ds(SIDE, SIDE), :] = jnp.where(lane < shift, turned, 0.0)
        patch_re, patch_im = patches[slot, 0], patches[slot, 1]
        pieces = (
            patch_re * back_re + patch_im * back_im,
            patch_re * back_im - patch_im * back_re,
        )
        for at in range(COMP):
            for plane in range(2):
                where_at = pl.ds((2 * at + plane) * SIDE, SIDE)
                terms[where_at, :] = terms[where_at, :] + weights_ref[slot, at] * pieces[plane]

    stages = (forward, relay_power, make_factor, relay_factor, backward)

    def step(at, carry):
        for lag, stage in enumerate(stages):

            @pl.when((at >= lag) & (at < SLOTS + lag))
            def _():
                stage(at - lag)

        return carry

    lax.fori_loop(0, SLOTS + len(stages) - 1, step, 0)

    def gathered(plane, tile_at, start):
        total = None
        for slot in range(SLOTS):
            row, base, shift = place_of(slot)
            index = jnp.where(
                tile_at == base, 2 * slot, jnp.where(tile_at == base + 1, 2 * slot + 1, EMPTY)
            )
            value = placed[plane, index, pl.ds(start - row, SIDE), :]
            total = value if total is None else total + value
        return total

    order = ((2, 0), (2, 1), (1, 1), (3, 0), (1, 0), (3, 1), (0, 0), (0, 1))

    def block_of(at):
        turn, plane = order[at]
        return lax.rem(mode + turn, MODES), plane

    rims = []
    for at in range(8):
        block, plane = block_of(at)
        for half in range(2):
            rim_out[at, half] = gathered(plane, 2 * block + half, 2 * SIDE)
        copy = send(rim_out.at[at], rim_in.at[at], rim_sems.at[:, at], {"tile": below})
        copy.start()
        rims.append(copy)

    def chunk_rows(at):
        return pl.ds(pl.multiple_of(at * rows, 8), rows)

    spread = [
        send(
            terms.at[chunk_rows(lax.rem(mine + step, group))],
            near_buf.at[step],
            near_sems.at[:, step],
            {"tile": near(step)},
        )
        for step in range(1, group)
    ]
    for copy in spread:
        copy.start()

    part_peers = ({"mode": right}, {"mode": left})
    part_kind = (0, 2, 1, 3, 4, 5)
    part_side = (0, 1, 0, 1, 0, 1)
    parts = [
        send(
            part.at[at],
            part_in.at[part_kind[at]],
            part_sems.at[:, part_kind[at]],
            part_peers[part_side[at]],
        )
        for at in range(6)
    ]
    arrivals = {part_kind[at]: parts[at] for at in range(6)}

    def whole(at, extra):
        block, plane = block_of(at)
        rims[at].wait_recv()
        for kind in extra:
            arrivals[kind].wait_recv()
        for half in range(2):
            value = gathered(plane, 2 * block + half, SIDE)
            value = value + jnp.where(tile > 0, rim_in[at, half], 0.0)
            for kind in extra:
                value = value + part_in[kind, half]
            yield half, value

    for at in range(4):
        for half, value in whole(at, ()):
            part[at, half] = value
        parts[at].start()

    for copy in spread:
        copy.wait_recv()
    total = terms[chunk_rows(mine), :]
    for step in range(1, group):
        total = total + near_buf[step]
    chunk[...] = total

    def to_owner(step):
        target = lax.rem(level + step, depth)
        at = pl.ds(pl.multiple_of(lax.rem(target, owners) * piece, 8), piece)
        return target, send(
            chunk.at[at], far_buf.at[step], far_sems.at[:, step], {"tile": beyond(step)}
        )

    def from_owner(source, step):
        at = pl.ds(pl.multiple_of(mine * rows + lax.rem(source, owners) * piece, 8), piece)
        return send(
            probe_out.at[at], probe_out.at[at], back_sems.at[:, step], {"tile": beyond(step)}
        )

    for step in range(1, depth):
        target, copy = to_owner(step)

        @pl.when(target < owners)
        def _():
            copy.start()

    for at in range(4, 6):
        for half, value in whole(at, (2 * (at - 4),)):
            part[at, half] = value
        parts[at].start()

    @pl.when(level < owners)
    def _():
        for step in range(1, depth):
            to_owner(step)[1].wait_recv()
        total = chunk[pl.ds(pl.multiple_of(lax.rem(level, owners) * piece, 8), piece), :]
        for step in range(1, depth):
            total = total + far_buf[step]
        at = pl.ds(pl.multiple_of(mine * rows + lax.rem(level, owners) * piece, 8), piece)
        probe_out[at, :] = total
        for step in range(1, depth):
            from_owner(level, step).start()

    for step in range(1, depth):
        source = lax.rem(level - step + depth, depth)

        @pl.when(source < owners)
        def _():
            from_owner(source, step).wait_recv()

    def shared(source, step):
        at = chunk_rows(source)
        return send(
            probe_out.at[at], probe_out.at[at], spread_sems.at[:, step], {"tile": near(step)}
        )

    for step in range(1, group):
        shared(mine, step).start()

    for at in range(6, 8):
        for half, value in whole(at, (4, 3) if at == 6 else (5, 1)):
            object_out[at - 6, :, pl.ds(half * SIDE, SIDE)] = value

    for step in range(1, group):
        shared(lax.rem(mine - step + group, group), step).wait_recv()

    for copy in halo + rims + parts + spread:
        copy.wait_send()
    for step in range(1, group):
        shared(mine, step).wait_send()
    for step in range(1, depth):
        target, copy = to_owner(step)

        @pl.when(target < owners)
        def _():
            copy.wait_send()

    @pl.when(level < owners)
    def _():
        for step in range(1, depth):
            from_owner(level, step).wait_send()

    def settle(slot, carry):
        for make in (first_pass, second_pass, third_pass, fourth_pass):
            for copy in make(slot):
                copy.wait_send()
        return carry

    lax.fori_loop(0, SLOTS, settle, 0)


def tables():
    line = np.arange(SIDE)
    angle = (line[:, None] * line[None, :] % SIDE) * (2.0 * math.pi / SIDE)
    cos = np.cos(angle) / math.sqrt(SIDE)
    sin = -np.sin(angle) / math.sqrt(SIDE)
    row = np.block([[cos, sin], [-sin, cos]])
    kinds = []
    for full in (row, row.T):
        high = full.astype(np.float32).astype(jnp.bfloat16)
        low = (full - high.astype(np.float64)).astype(np.float32).astype(jnp.bfloat16)
        kinds += [high, low]
    return kinds


def local(object_field, components, relax_weights, amplitudes, positions, counts):
    tiles = lax.axis_size("tile")
    group = group_size(tiles)
    depth = tiles // group
    rows = COMP * 2 * SIDE // group
    piece = rows // owner_count(depth)
    f32 = jnp.float32
    anywhere = pl.BlockSpec(memory_space=pl.ANY)
    scalars = pl.BlockSpec(memory_space=pltpu.SMEM)
    vector = pl.BlockSpec(memory_space=pltpu.VMEM)
    flops = 2 * 2 * SLOTS * 3 * 2 * 256 * 256 * 128
    object_grad, probe_grad = pl.pallas_call(
        functools.partial(kernel, tiles),
        out_shape=(
            jax.ShapeDtypeStruct((2, SIDE, 2 * SIDE), f32),
            jax.ShapeDtypeStruct((COMP * 2 * SIDE, SIDE), f32),
        ),
        in_specs=[anywhere, anywhere, scalars, anywhere, scalars, scalars] + [vector] * 4,
        out_specs=(vector, vector),
        scratch_shapes=[
            pltpu.VMEM((2, TILES_WIDE, 2 * SIDE, SIDE), f32),
            pltpu.VMEM((COMP, 2, SIDE, SIDE), f32),
            pltpu.VMEM((SLOTS, QUARTER, SIDE), f32),
            pltpu.VMEM((SLOTS, 2, SIDE, SIDE), f32),
            pltpu.VMEM((SLOTS, 2, SIDE, SIDE), f32),
            pltpu.VMEM((SLOTS, 2 * SIDE, SIDE), f32),
            pltpu.VMEM((SLOTS, SIDE + HALF, SIDE), f32),
            pltpu.VMEM((SLOTS, 2, QUARTER, SIDE), f32),
            pltpu.VMEM((SLOTS, 2, HALF, SIDE), f32),
            pltpu.VMEM((SLOTS, 2, HALF, SIDE), f32),
            pltpu.VMEM((SLOTS, SIDE, SIDE), f32),
            pltpu.VMEM((2, EMPTY + 1, 3 * SIDE, SIDE), f32),
            pltpu.VMEM((8, 2, SIDE, SIDE), f32),
            pltpu.VMEM((8, 2, SIDE, SIDE), f32),
            pltpu.VMEM((6, 2, SIDE, SIDE), f32),
            pltpu.VMEM((6, 2, SIDE, SIDE), f32),
            pltpu.VMEM((COMP * 2 * SIDE, SIDE), f32),
            pltpu.VMEM((rows, SIDE), f32),
            pltpu.VMEM((group, rows, SIDE), f32),
            pltpu.VMEM((depth, piece, SIDE), f32),
            pltpu.SemaphoreType.DMA((2 + TILES_WIDE,)),
            pltpu.SemaphoreType.DMA((2, TILES_WIDE)),
            pltpu.SemaphoreType.DMA((2, SLOTS, 8)),
            pltpu.SemaphoreType.DMA((2, 8)),
            pltpu.SemaphoreType.DMA((2, 6)),
            pltpu.SemaphoreType.DMA((2, group)),
            pltpu.SemaphoreType.DMA((2, depth)),
            pltpu.SemaphoreType.DMA((2, depth)),
            pltpu.SemaphoreType.DMA((2, group)),
        ],
        compiler_params=pltpu.CompilerParams(
            collective_id=0, has_side_effects=True, vmem_limit_bytes=48 * 1024 * 1024
        ),
        cost_estimate=pl.CostEstimate(
            flops=flops, bytes_accessed=4 * 1024 * 1024, transcendentals=SLOTS * SIDE * SIDE
        ),
    )(
        object_field,
        components,
        relax_weights,
        amplitudes,
        positions,
        counts,
        *[jnp.asarray(table) for table in tables()],
    )
    return object_grad, probe_grad.reshape(1, COMP, 2, SIDE, SIDE)


def solution(mesh):
    return jax.shard_map(
        local,
        mesh=mesh,
        in_specs=(
            P(None, "tile", None),
            P("mode", None, None, None, None),
            P("tile", None),
            P("tile", None, None),
            P("tile", None),
            P("tile"),
        ),
        out_specs=(P(None, "tile", "mode"), P("mode", None, None, None, None)),
        check_vma=False,
    )
```

```python
import functools
import math

import jax
import jax.numpy as jnp
import numpy as np
from jax import lax
from jax.experimental import pallas as pl
from jax.experimental.pallas import tpu as pltpu
from jax.sharding import PartitionSpec as P

MESH = pl.DeviceIdType.MESH
SIDE = 128
SLOTS = 8
COMP = 4
MODES = 4
TILES_WIDE = 8
QUARTER = 32
HALF = 16
EMPTY = 2 * SLOTS
PACK = 1
PACKS = SLOTS // PACK
LAG = 5


def group_size(tiles):
    return 8 if tiles % 16 == 0 else 2


def owner_count(depth):
    return 1 << (depth.bit_length() - 1)


def split(values):
    high = values.astype(jnp.bfloat16)
    low = (values - high.astype(jnp.float32)).astype(jnp.bfloat16)
    return high, low


def dot(left, right):
    return jnp.dot(left, right, preferred_element_type=jnp.float32)


def both_sides(wide, right_high, right_low, left_high, left_low):
    high, low = split(wide)
    middle = dot(high, right_high) + dot(low, right_high) + dot(high, right_low)
    tall = jnp.concatenate([middle[:, :SIDE], middle[:, SIDE:]], axis=0)
    high, low = split(tall)
    return dot(left_high, high) + dot(left_high, low) + dot(left_low, high)


def kernel(
    tiles,
    object_ref,
    components_ref,
    weights_ref,
    amplitudes_ref,
    positions_ref,
    counts_ref,
    table_ref,
    object_out,
    probe_out,
    weights,
    positions,
    counts,
    table,
    waves,
    ext,
    comp,
    amps,
    patches,
    probes,
    far,
    power,
    pair_in,
    pair_mid,
    pair_sum,
    factor,
    placed,
    rim_out,
    rim_in,
    part,
    part_in,
    terms,
    chunk,
    near_buf,
    far_buf,
    local_sems,
    halo_sems,
    slot_sems,
    rim_sems,
    part_sems,
    near_sems,
    far_sems,
    back_sems,
    spread_sems,
):
    group = group_size(tiles)
    depth = tiles // group
    owners = owner_count(depth)
    rows = COMP * 2 * SIDE // group
    piece = rows // owners
    tile = lax.axis_index("tile")
    mode = lax.axis_index("mode")
    above = lax.rem(tile + tiles - 1, tiles)
    below = lax.rem(tile + 1, tiles)
    right = lax.rem(mode + 1, MODES)
    left = lax.rem(mode + MODES - 1, MODES)
    mine = lax.rem(tile, group)
    level = lax.div(tile, group)

    def near(step):
        return level * group + lax.rem(mine + step, group)

    def beyond(step):
        return lax.rem(level + step, depth) * group + mine

    def send(src, dst, sems, peer):
        return pltpu.make_async_remote_copy(
            src_ref=src,
            dst_ref=dst,
            send_sem=sems.at[0],
            recv_sem=sems.at[1],
            device_id=peer,
            device_id_type=MESH,
        )

    def columns(ref, at):
        return ref.at[:, :, pl.ds(at * SIDE, SIDE)]

    barrier = pltpu.get_barrier_semaphore()
    peers = [{"tile": above}, {"tile": below}, {"mode": right}, {"mode": left}]
    peers += [{"tile": near(step)} for step in range(1, group)]
    peers += [{"tile": beyond(step)} for step in range(1, depth)]
    for peer in peers:
        pl.semaphore_signal(barrier, inc=1, device_id=peer, device_id_type=MESH)
    loads = [
        pltpu.make_async_copy(weights_ref, weights, local_sems.at[10]),
        pltpu.make_async_copy(positions_ref, positions, local_sems.at[11]),
        pltpu.make_async_copy(counts_ref, counts, local_sems.at[12]),
        pltpu.make_async_copy(table_ref, waves, local_sems.at[13]),
        pltpu.make_async_copy(components_ref.at[0], comp, local_sems.at[0]),
        pltpu.make_async_copy(
            amplitudes_ref.at[:, pl.ds(pl.multiple_of(mode * QUARTER, 8), QUARTER), :],
            amps,
            local_sems.at[1],
        ),
    ] + [
        pltpu.make_async_copy(
            columns(object_ref, at), ext.at[:, at, pl.ds(0, SIDE), :], local_sems.at[2 + at]
        )
        for at in range(TILES_WIDE)
    ]
    for copy in loads:
        copy.start()
    pl.semaphore_wait(barrier, len(peers))

    halo = [
        send(
            columns(object_ref, at),
            ext.at[:, at, pl.ds(SIDE, SIDE), :],
            halo_sems.at[:, at],
            {"tile": above},
        )
        for at in range(TILES_WIDE)
    ]
    for copy in halo:
        copy.start()

    terms[...] = jnp.zeros_like(terms)

    def clear(at, carry):
        for plane in range(2):
            placed[plane, at, pl.ds(0, SIDE), :] = jnp.zeros((SIDE, SIDE), jnp.float32)
            placed[plane, at, pl.ds(2 * SIDE, SIDE), :] = jnp.zeros((SIDE, SIDE), jnp.float32)
        return carry

    lax.fori_loop(0, EMPTY + 1, clear, 0)
    for plane in range(2):
        placed[plane, EMPTY, pl.ds(SIDE, SIDE), :] = jnp.zeros((SIDE, SIDE), jnp.float32)
    for copy in loads:
        copy.wait()
    cos_high, cos_low = split(waves[0])
    sin_high, sin_low = split(waves[1])
    for at, (cos, sin) in enumerate(((cos_high, sin_high), (cos_low, sin_low))):
        lower = jnp.concatenate([-sin, cos], axis=1)
        upper = jnp.concatenate([cos, sin], axis=1)
        table[at] = jnp.concatenate([upper, lower], axis=0)
        lower = jnp.concatenate([sin, cos], axis=1)
        upper = jnp.concatenate([cos, -sin], axis=1)
        table[2 + at] = jnp.concatenate([upper, lower], axis=0)

    def mix(slot, carry):
        for plane in range(2):
            total = weights[0, slot] * comp[0, plane]
            for at in range(1, COMP):
                total = total + weights[at, slot] * comp[at, plane]
            probes[slot, plane] = total
        return carry

    lax.fori_loop(0, SLOTS, mix, 0)
    for copy in halo:
        copy.wait_recv()

    @pl.when(tile == tiles - 1)
    def _():
        for plane in range(2):
            for at in range(TILES_WIDE):
                ext[plane, at, pl.ds(SIDE, SIDE), :] = jnp.zeros((SIDE, SIDE), jnp.float32)

    lane = lax.broadcasted_iota(jnp.int32, (SIDE, SIDE), 1)

    def place_of(slot):
        row = positions[0, slot] & (SIDE - 1)
        col = positions[1, slot]
        base = jnp.minimum(lax.shift_right_logical(col, 7), TILES_WIDE - 2)
        return row, base, col - base * SIDE

    def take(slot, plane):
        row, base, shift = place_of(slot)
        turn = (SIDE - shift) & (SIDE - 1)
        first = pltpu.roll(ext[plane, base, pl.ds(row, SIDE), :], turn, 1)
        second = pltpu.roll(ext[plane, base + 1, pl.ds(row, SIDE), :], turn, 1)
        return jnp.where(lane < SIDE - shift, first, second)

    ahead = pl.multiple_of(lax.rem(QUARTER * (mode + 1) + HALF, SIDE), 8)
    behind = pl.multiple_of(lax.rem(QUARTER * (mode + 2) + HALF, SIDE), 8)
    own_rows = pl.multiple_of(QUARTER * mode, 8)
    right_rows = pl.multiple_of(QUARTER * right, 8)
    left_rows = pl.multiple_of(QUARTER * left, 8)

    def slots_of(pack):
        return pl.ds(pack * PACK, PACK)

    def first_pass(pack):
        return [
            send(
                power.at[slots_of(pack), pl.ds(ahead, QUARTER), :],
                pair_in.at[pack, 0],
                slot_sems.at[:, pack, 0],
                {"mode": right},
            ),
            send(
                power.at[slots_of(pack), pl.ds(behind, QUARTER), :],
                pair_in.at[pack, 1],
                slot_sems.at[:, pack, 1],
                {"mode": left},
            ),
        ]

    def second_pass(pack):
        return [
            send(
                pair_mid.at[pack, 0],
                pair_sum.at[pack, 0],
                slot_sems.at[:, pack, 2],
                {"mode": right},
            ),
            send(
                pair_mid.at[pack, 1],
                pair_sum.at[pack, 1],
                slot_sems.at[:, pack, 3],
                {"mode": left},
            ),
        ]

    def in_place(pack, start, count, kind, peer):
        ref = factor.at[slots_of(pack), pl.ds(start, count), :]
        return send(ref, ref, slot_sems.at[:, pack, kind], {"mode": peer})

    def third_pass(pack, start_right=own_rows, start_left=own_rows):
        return [
            in_place(pack, start_right, QUARTER, 4, right),
            in_place(pack, start_left, QUARTER, 5, left),
        ]

    def fourth_pass(pack, top=left_rows, bottom=right_rows):
        return [
            in_place(pack, top, HALF, 6, right),
            in_place(pack, pl.multiple_of(bottom + HALF, 8), HALF, 7, left),
        ]

    def forward(slot, carry):
        for plane in range(2):
            patches[slot, plane] = take(slot, plane)
        probe_re, probe_im = probes[slot, 0], probes[slot, 1]
        patch_re, patch_im = patches[slot, 0], patches[slot, 1]
        wide = jnp.concatenate(
            [
                probe_re * patch_re - probe_im * patch_im,
                probe_re * patch_im + probe_im * patch_re,
            ],
            axis=1,
        )
        wave = both_sides(wide, table[0], table[1], table[2], table[3])
        far[slot] = wave
        strength = wave[:SIDE] * wave[:SIDE] + wave[SIDE:] * wave[SIDE:]
        power[slot, pl.ds(0, SIDE), :] = strength
        power[slot, pl.ds(SIDE, HALF), :] = strength[:HALF]
        return carry

    def send_power(pack):
        lax.fori_loop(pack * PACK, pack * PACK + PACK, forward, 0)
        for copy in first_pass(pack):
            copy.start()

    def relay_power(pack):
        slots = slots_of(pack)
        to_right, to_left = first_pass(pack)
        go_right, go_left = second_pass(pack)
        to_right.wait_recv()
        pair_mid[pack, 0] = (
            pair_in[pack, 0, :, pl.ds(HALF, HALF), :] + power[slots, pl.ds(right_rows, HALF), :]
        )
        go_right.start()
        to_left.wait_recv()
        pair_mid[pack, 1] = (
            pair_in[pack, 1, :, pl.ds(0, HALF), :]
            + power[slots, pl.ds(pl.multiple_of(left_rows + HALF, 8), HALF), :]
        )
        go_left.start()

    def make_factor(pack):
        for copy in second_pass(pack):
            copy.wait_recv()
        for inner in range(PACK):
            slot = pack * PACK + inner
            own = power[slot, pl.ds(own_rows, QUARTER), :]
            top = own[:HALF] + pair_sum[pack, 0, inner] + pair_in[pack, 1, inner, pl.ds(HALF, HALF), :]
            bottom = own[HALF:] + pair_sum[pack, 1, inner] + pair_in[pack, 0, inner, pl.ds(0, HALF), :]
            intensity = jnp.concatenate([top, bottom], axis=0)
            ratio = 1.0 - amps[slot] * lax.rsqrt(jnp.maximum(intensity, 1.0))
            factor[slot, pl.ds(own_rows, QUARTER), :] = jnp.where(slot < counts[0], ratio, 0.0)
        for copy in third_pass(pack):
            copy.start()

    def relay_factor(pack):
        from_left, from_right = third_pass(pack, left_rows, right_rows)
        go_right, go_left = fourth_pass(pack)
        from_left.wait_recv()
        go_right.start()
        from_right.wait_recv()
        go_left.start()

    def backward(slot, carry):
        scale = factor[slot]
        wave = far[slot]
        wide = jnp.concatenate([wave[:SIDE] * scale, wave[SIDE:] * scale], axis=1)
        back = both_sides(wide, table[2], table[3], table[0], table[1])
        back_re, back_im = back[:SIDE], back[SIDE:]
        probe_re, probe_im = probes[slot, 0], probes[slot, 1]
        shift = place_of(slot)[2]
        grads = (
            probe_re * back_re + probe_im * back_im,
            probe_re * back_im - probe_im * back_re,
        )
        for plane in range(2):
            turned = pltpu.roll(grads[plane], shift & (SIDE - 1), 1)
            placed[plane, 2 * slot, pl.ds(SIDE, SIDE), :] = jnp.where(lane >= shift, turned, 0.0)
            placed[plane, 2 * slot + 1, pl.ds(SIDE, SIDE), :] = jnp.where(lane < shift, turned, 0.0)
        patch_re, patch_im = patches[slot, 0], patches[slot, 1]
        pieces = (
            patch_re * back_re + patch_im * back_im,
            patch_re * back_im - patch_im * back_re,
        )
        for at in range(COMP):
            for plane in range(2):
                where_at = pl.ds((2 * at + plane) * SIDE, SIDE)
                terms[where_at, :] = terms[where_at, :] + weights[at, slot] * pieces[plane]
        return carry

    def use_factor(pack):
        across = pl.multiple_of(QUARTER * lax.rem(mode + 2, MODES), 8)
        for copy in fourth_pass(pack, across, across):
            copy.wait_recv()
        lax.fori_loop(pack * PACK, pack * PACK + PACK, backward, 0)

    stages = (send_power, relay_power, make_factor, relay_factor, use_factor)

    def step(at, carry):
        for place, stage in enumerate(stages):
            lag = place * LAG

            @pl.when((at >= lag) & (at < PACKS + lag))
            def _():
                stage(at - lag)

        return carry

    lax.fori_loop(0, PACKS + (len(stages) - 1) * LAG, step, 0)

    def gathered(plane, tile_at, start):
        total = None
        for slot in range(SLOTS):
            row, base, shift = place_of(slot)
            index = jnp.where(
                tile_at == base, 2 * slot, jnp.where(tile_at == base + 1, 2 * slot + 1, EMPTY)
            )
            value = placed[plane, index, pl.ds(start - row, SIDE), :]
            total = value if total is None else total + value
        return total

    order = ((2, 0), (2, 1), (1, 1), (3, 0), (1, 0), (3, 1), (0, 0), (0, 1))

    def block_of(at):
        turn, plane = order[at]
        return lax.rem(mode + turn, MODES), plane

    rims = []
    for at in range(8):
        block, plane = block_of(at)
        for half in range(2):
            rim_out[at, half] = gathered(plane, 2 * block + half, 2 * SIDE)
        copy = send(rim_out.at[at], rim_in.at[at], rim_sems.at[:, at], {"tile": below})
        copy.start()
        rims.append(copy)

    def chunk_rows(at):
        return pl.ds(pl.multiple_of(at * rows, 8), rows)

    spread = [
        send(
            terms.at[chunk_rows(lax.rem(mine + step, group))],
            near_buf.at[step],
            near_sems.at[:, step],
            {"tile": near(step)},
        )
        for step in range(1, group)
    ]
    for copy in spread:
        copy.start()

    part_peers = ({"mode": right}, {"mode": left})
    part_kind = (0, 2, 1, 3, 4, 5)
    part_side = (0, 1, 0, 1, 0, 1)
    parts = [
        send(
            part.at[at],
            part_in.at[part_kind[at]],
            part_sems.at[:, part_kind[at]],
            part_peers[part_side[at]],
        )
        for at in range(6)
    ]
    arrivals = {part_kind[at]: parts[at] for at in range(6)}

    def whole(at, extra):
        block, plane = block_of(at)
        rims[at].wait_recv()
        for kind in extra:
            arrivals[kind].wait_recv()
        for half in range(2):
            value = gathered(plane, 2 * block + half, SIDE)
            value = value + jnp.where(tile > 0, rim_in[at, half], 0.0)
            for kind in extra:
                value = value + part_in[kind, half]
            yield half, value

    for at in range(4):
        for half, value in whole(at, ()):
            part[at, half] = value
        parts[at].start()

    for copy in spread:
        copy.wait_recv()
    total = terms[chunk_rows(mine), :]
    for step in range(1, group):
        total = total + near_buf[step]
    chunk[...] = total

    def to_owner(step):
        target = lax.rem(level + step, depth)
        at = pl.ds(pl.multiple_of(lax.rem(target, owners) * piece, 8), piece)
        return target, send(
            chunk.at[at], far_buf.at[step], far_sems.at[:, step], {"tile": beyond(step)}
        )

    def from_owner(source, step):
        at = pl.ds(pl.multiple_of(mine * rows + lax.rem(source, owners) * piece, 8), piece)
        return send(
            probe_out.at[at], probe_out.at[at], back_sems.at[:, step], {"tile": beyond(step)}
        )

    for step in range(1, depth):
        target, copy = to_owner(step)

        @pl.when(target < owners)
        def _():
            copy.start()

    for at in range(4, 6):
        for half, value in whole(at, (2 * (at - 4),)):
            part[at, half] = value
        parts[at].start()

    @pl.when(level < owners)
    def _():
        for step in range(1, depth):
            to_owner(step)[1].wait_recv()
        total = chunk[pl.ds(pl.multiple_of(lax.rem(level, owners) * piece, 8), piece), :]
        for step in range(1, depth):
            total = total + far_buf[step]
        at = pl.ds(pl.multiple_of(mine * rows + lax.rem(level, owners) * piece, 8), piece)
        probe_out[at, :] = total
        for step in range(1, depth):
            from_owner(level, step).start()

    for step in range(1, depth):
        source = lax.rem(level - step + depth, depth)

        @pl.when(source < owners)
        def _():
            from_owner(source, step).wait_recv()

    def shared(source, step):
        at = chunk_rows(source)
        return send(
            probe_out.at[at], probe_out.at[at], spread_sems.at[:, step], {"tile": near(step)}
        )

    for step in range(1, group):
        shared(mine, step).start()

    for at in range(6, 8):
        for half, value in whole(at, (4, 3) if at == 6 else (5, 1)):
            object_out[at - 6, :, pl.ds(half * SIDE, SIDE)] = value

    for step in range(1, group):
        shared(lax.rem(mine - step + group, group), step).wait_recv()

    for copy in halo + rims + parts + spread:
        copy.wait_send()
    for step in range(1, group):
        shared(mine, step).wait_send()
    for step in range(1, depth):
        target, copy = to_owner(step)

        @pl.when(target < owners)
        def _():
            copy.wait_send()

    @pl.when(level < owners)
    def _():
        for step in range(1, depth):
            from_owner(level, step).wait_send()

    def settle(pack, carry):
        for make in (first_pass, second_pass, third_pass, fourth_pass):
            for copy in make(pack):
                copy.wait_send()
        return carry

    lax.fori_loop(0, PACKS, settle, 0)


def tables():
    line = np.arange(SIDE)
    angle = (line[:, None] * line[None, :] % SIDE) * (2.0 * math.pi / SIDE)
    cos = np.cos(angle) / math.sqrt(SIDE)
    sin = -np.sin(angle) / math.sqrt(SIDE)
    return np.stack([cos, sin]).astype(np.float32)


def local(object_field, components, relax_weights, amplitudes, positions, counts):
    tiles = lax.axis_size("tile")
    group = group_size(tiles)
    depth = tiles // group
    rows = COMP * 2 * SIDE // group
    piece = rows // owner_count(depth)
    f32 = jnp.float32
    anywhere = pl.BlockSpec(memory_space=pltpu.HBM)
    vector = pl.BlockSpec(memory_space=pltpu.VMEM)
    flops = 2 * 2 * SLOTS * 3 * 2 * 256 * 256 * 128
    object_grad, probe_grad = pl.pallas_call(
        functools.partial(kernel, tiles),
        out_shape=(
            jax.ShapeDtypeStruct((2, SIDE, 2 * SIDE), f32),
            jax.ShapeDtypeStruct((COMP * 2 * SIDE, SIDE), f32),
        ),
        in_specs=[anywhere] * 7,
        out_specs=(vector, vector),
        scratch_shapes=[
            pltpu.SMEM((COMP, SLOTS), f32),
            pltpu.SMEM((2, SLOTS), jnp.int32),
            pltpu.SMEM((1,), jnp.int32),
            pltpu.VMEM((4, 2 * SIDE, 2 * SIDE), jnp.bfloat16),
            pltpu.VMEM((2, SIDE, SIDE), f32),
            pltpu.VMEM((2, TILES_WIDE, 2 * SIDE, SIDE), f32),
            pltpu.VMEM((COMP, 2, SIDE, SIDE), f32),
            pltpu.VMEM((SLOTS, QUARTER, SIDE), f32),
            pltpu.VMEM((SLOTS, 2, SIDE, SIDE), f32),
            pltpu.VMEM((SLOTS, 2, SIDE, SIDE), f32),
            pltpu.VMEM((SLOTS, 2 * SIDE, SIDE), f32),
            pltpu.VMEM((SLOTS, SIDE + HALF, SIDE), f32),
            pltpu.VMEM((PACKS, 2, PACK, QUARTER, SIDE), f32),
            pltpu.VMEM((PACKS, 2, PACK, HALF, SIDE), f32),
            pltpu.VMEM((PACKS, 2, PACK, HALF, SIDE), f32),
            pltpu.VMEM((SLOTS, SIDE, SIDE), f32),
            pltpu.VMEM((2, EMPTY + 1, 3 * SIDE, SIDE), f32),
            pltpu.VMEM((8, 2, SIDE, SIDE), f32),
            pltpu.VMEM((8, 2, SIDE, SIDE), f32),
            pltpu.VMEM((6, 2, SIDE, SIDE), f32),
            pltpu.VMEM((6, 2, SIDE, SIDE), f32),
            pltpu.VMEM((COMP * 2 * SIDE, SIDE), f32),
            pltpu.VMEM((rows, SIDE), f32),
            pltpu.VMEM((group, rows, SIDE), f32),
            pltpu.VMEM((depth, piece, SIDE), f32),
            pltpu.SemaphoreType.DMA((6 + TILES_WIDE,)),
            pltpu.SemaphoreType.DMA((2, TILES_WIDE)),
            pltpu.SemaphoreType.DMA((2, PACKS, 8)),
            pltpu.SemaphoreType.DMA((2, 8)),
            pltpu.SemaphoreType.DMA((2, 6)),
            pltpu.SemaphoreType.DMA((2, group)),
            pltpu.SemaphoreType.DMA((2, depth)),
            pltpu.SemaphoreType.DMA((2, depth)),
            pltpu.SemaphoreType.DMA((2, group)),
        ],
        compiler_params=pltpu.CompilerParams(
            collective_id=0, has_side_effects=True, vmem_limit_bytes=62 * 1024 * 1024
        ),
        cost_estimate=pl.CostEstimate(
            flops=flops, bytes_accessed=4 * 1024 * 1024, transcendentals=SLOTS * SIDE * SIDE
        ),
    )(
        object_field,
        components,
        relax_weights.T,
        amplitudes,
        positions.T,
        counts,
        jnp.asarray(tables()),
    )
    return object_grad, probe_grad.reshape(1, COMP, 2, SIDE, SIDE)


def solution(mesh):
    return jax.shard_map(
        local,
        mesh=mesh,
        in_specs=(
            P(None, "tile", None),
            P("mode", None, None, None, None),
            P("tile", None),
            P("tile", None, None),
            P("tile", None),
            P("tile"),
        ),
        out_specs=(P(None, "tile", "mode"), P("mode", None, None, None, None)),
        check_vma=False,
    )
```

```python
import functools
import math

import jax
import jax.numpy as jnp
import numpy as np
from jax import lax
from jax.experimental import pallas as pl
from jax.experimental.pallas import tpu as pltpu
from jax.sharding import PartitionSpec as P

MESH = pl.DeviceIdType.MESH
SIDE = 128
SLOTS = 8
COMP = 4
MODES = 4
TILES_WIDE = 8
QUARTER = 32
HALF = 16
EMPTY = 2 * SLOTS
PACK = 2
PACKS = SLOTS // PACK
LAG = 3


def group_size(tiles):
    return 8 if tiles % 16 == 0 else 4


def owner_count(depth):
    return 1 << (depth.bit_length() - 1)


def split(values):
    high = values.astype(jnp.bfloat16)
    low = (values - high.astype(jnp.float32)).astype(jnp.bfloat16)
    return high, low


def dot(left, right):
    return jnp.dot(left, right, preferred_element_type=jnp.float32)


def both_sides(wide, right_high, right_low, left_high, left_low):
    high, low = split(wide)
    middle = dot(high, right_high) + dot(low, right_high) + dot(high, right_low)
    tall = jnp.concatenate([middle[:, :SIDE], middle[:, SIDE:]], axis=0)
    high, low = split(tall)
    return dot(left_high, high) + dot(left_high, low) + dot(left_low, high)


def kernel(
    tiles,
    object_ref,
    components_ref,
    weights_ref,
    amplitudes_ref,
    positions_ref,
    counts_ref,
    table_ref,
    object_out,
    probe_out,
    weights,
    positions,
    counts,
    table,
    waves,
    ext,
    comp,
    amps,
    patches,
    probes,
    far,
    power,
    pair_in,
    pair_mid,
    pair_sum,
    factor,
    placed,
    rim_out,
    rim_in,
    part,
    part_in,
    terms,
    half_in,
    half_sum,
    chunk,
    near_buf,
    far_buf,
    local_sems,
    halo_sems,
    slot_sems,
    rim_sems,
    part_sems,
    pair_sems,
    near_sems,
    far_sems,
    back_sems,
    spread_sems,
):
    group = group_size(tiles)
    depth = tiles // group
    owners = owner_count(depth)
    rows = COMP * 2 * SIDE // group
    piece = rows // owners
    tile = lax.axis_index("tile")
    mode = lax.axis_index("mode")
    above = lax.rem(tile + tiles - 1, tiles)
    below = lax.rem(tile + 1, tiles)
    right = lax.rem(mode + 1, MODES)
    left = lax.rem(mode + MODES - 1, MODES)
    mine = lax.rem(tile, group)
    level = lax.div(tile, group)

    across = group // 2
    core = lax.rem(mine, 2)
    chip = lax.div(mine, 2)
    place = core * across + chip
    sibling = level * group + chip * 2 + 1 - core
    half_rows = COMP * SIDE

    def near(step):
        return level * group + lax.rem(chip + step, across) * 2 + core

    def beyond(step):
        return lax.rem(level + step, depth) * group + mine

    def send(src, dst, sems, peer):
        return pltpu.make_async_remote_copy(
            src_ref=src,
            dst_ref=dst,
            send_sem=sems.at[0],
            recv_sem=sems.at[1],
            device_id=peer,
            device_id_type=MESH,
        )

    def columns(ref, at):
        return ref.at[:, :, pl.ds(at * SIDE, SIDE)]

    barrier = pltpu.get_barrier_semaphore()
    peers = [{"tile": above}, {"tile": below}, {"mode": right}, {"mode": left}]
    peers += [{"tile": sibling}]
    peers += [{"tile": near(step)} for step in range(1, across)]
    peers += [{"tile": beyond(step)} for step in range(1, depth)]
    for peer in peers:
        pl.semaphore_signal(barrier, inc=1, device_id=peer, device_id_type=MESH)
    loads = [
        pltpu.make_async_copy(weights_ref, weights, local_sems.at[10]),
        pltpu.make_async_copy(positions_ref, positions, local_sems.at[11]),
        pltpu.make_async_copy(counts_ref, counts, local_sems.at[12]),
        pltpu.make_async_copy(table_ref, waves, local_sems.at[13]),
        pltpu.make_async_copy(components_ref.at[0], comp, local_sems.at[0]),
        pltpu.make_async_copy(
            amplitudes_ref.at[:, pl.ds(pl.multiple_of(mode * QUARTER, 8), QUARTER), :],
            amps,
            local_sems.at[1],
        ),
    ] + [
        pltpu.make_async_copy(
            columns(object_ref, at), ext.at[:, at, pl.ds(0, SIDE), :], local_sems.at[2 + at]
        )
        for at in range(TILES_WIDE)
    ]
    for copy in loads:
        copy.start()
    pl.semaphore_wait(barrier, len(peers))

    halo = [
        send(
            columns(object_ref, at),
            ext.at[:, at, pl.ds(SIDE, SIDE), :],
            halo_sems.at[:, at],
            {"tile": above},
        )
        for at in range(TILES_WIDE)
    ]
    for copy in halo:
        copy.start()

    terms[...] = jnp.zeros_like(terms)

    def clear(at, carry):
        for plane in range(2):
            placed[plane, at, pl.ds(0, SIDE), :] = jnp.zeros((SIDE, SIDE), jnp.float32)
            placed[plane, at, pl.ds(2 * SIDE, SIDE), :] = jnp.zeros((SIDE, SIDE), jnp.float32)
        return carry

    lax.fori_loop(0, EMPTY + 1, clear, 0)
    for plane in range(2):
        placed[plane, EMPTY, pl.ds(SIDE, SIDE), :] = jnp.zeros((SIDE, SIDE), jnp.float32)
    for copy in loads:
        copy.wait()
    cos_high, cos_low = split(waves[0])
    sin_high, sin_low = split(waves[1])
    for at, (cos, sin) in enumerate(((cos_high, sin_high), (cos_low, sin_low))):
        lower = jnp.concatenate([-sin, cos], axis=1)
        upper = jnp.concatenate([cos, sin], axis=1)
        table[at] = jnp.concatenate([upper, lower], axis=0)
        lower = jnp.concatenate([sin, cos], axis=1)
        upper = jnp.concatenate([cos, -sin], axis=1)
        table[2 + at] = jnp.concatenate([upper, lower], axis=0)

    def mix(slot, carry):
        for plane in range(2):
            total = weights[0, slot] * comp[0, plane]
            for at in range(1, COMP):
                total = total + weights[at, slot] * comp[at, plane]
            probes[slot, plane] = total
        return carry

    lax.fori_loop(0, SLOTS, mix, 0)
    for copy in halo:
        copy.wait_recv()

    @pl.when(tile == tiles - 1)
    def _():
        for plane in range(2):
            for at in range(TILES_WIDE):
                ext[plane, at, pl.ds(SIDE, SIDE), :] = jnp.zeros((SIDE, SIDE), jnp.float32)

    lane = lax.broadcasted_iota(jnp.int32, (SIDE, SIDE), 1)

    def place_of(slot):
        row = positions[0, slot] & (SIDE - 1)
        col = positions[1, slot]
        base = jnp.minimum(lax.shift_right_logical(col, 7), TILES_WIDE - 2)
        return row, base, col - base * SIDE

    def take(slot, plane):
        row, base, shift = place_of(slot)
        turn = (SIDE - shift) & (SIDE - 1)
        first = pltpu.roll(ext[plane, base, pl.ds(row, SIDE), :], turn, 1)
        second = pltpu.roll(ext[plane, base + 1, pl.ds(row, SIDE), :], turn, 1)
        return jnp.where(lane < SIDE - shift, first, second)

    ahead = pl.multiple_of(lax.rem(QUARTER * (mode + 1) + HALF, SIDE), 8)
    behind = pl.multiple_of(lax.rem(QUARTER * (mode + 2) + HALF, SIDE), 8)
    own_rows = pl.multiple_of(QUARTER * mode, 8)
    right_rows = pl.multiple_of(QUARTER * right, 8)
    left_rows = pl.multiple_of(QUARTER * left, 8)

    def slots_of(pack):
        return pl.ds(pack * PACK, PACK)

    def first_pass(pack):
        return [
            send(
                power.at[slots_of(pack), pl.ds(ahead, QUARTER), :],
                pair_in.at[pack, 0],
                slot_sems.at[:, pack, 0],
                {"mode": right},
            ),
            send(
                power.at[slots_of(pack), pl.ds(behind, QUARTER), :],
                pair_in.at[pack, 1],
                slot_sems.at[:, pack, 1],
                {"mode": left},
            ),
        ]

    def second_pass(pack):
        return [
            send(
                pair_mid.at[pack, 0],
                pair_sum.at[pack, 0],
                slot_sems.at[:, pack, 2],
                {"mode": right},
            ),
            send(
                pair_mid.at[pack, 1],
                pair_sum.at[pack, 1],
                slot_sems.at[:, pack, 3],
                {"mode": left},
            ),
        ]

    def in_place(pack, start, count, kind, peer):
        ref = factor.at[slots_of(pack), pl.ds(start, count), :]
        return send(ref, ref, slot_sems.at[:, pack, kind], {"mode": peer})

    def third_pass(pack, start_right=own_rows, start_left=own_rows):
        return [
            in_place(pack, start_right, QUARTER, 4, right),
            in_place(pack, start_left, QUARTER, 5, left),
        ]

    def fourth_pass(pack, top=left_rows, bottom=right_rows):
        return [
            in_place(pack, top, HALF, 6, right),
            in_place(pack, pl.multiple_of(bottom + HALF, 8), HALF, 7, left),
        ]

    def forward(slot):
        for plane in range(2):
            patches[slot, plane] = take(slot, plane)
        probe_re, probe_im = probes[slot, 0], probes[slot, 1]
        patch_re, patch_im = patches[slot, 0], patches[slot, 1]
        wide = jnp.concatenate(
            [
                probe_re * patch_re - probe_im * patch_im,
                probe_re * patch_im + probe_im * patch_re,
            ],
            axis=1,
        )
        wave = both_sides(wide, table[0], table[1], table[2], table[3])
        far[slot] = wave
        strength = wave[:SIDE] * wave[:SIDE] + wave[SIDE:] * wave[SIDE:]
        power[slot, pl.ds(0, SIDE), :] = strength
        power[slot, pl.ds(SIDE, HALF), :] = strength[:HALF]

    def send_power(pack):
        for inner in range(PACK):
            forward(pack * PACK + inner)
        for copy in first_pass(pack):
            copy.start()

    def relay_power(pack):
        slots = slots_of(pack)
        to_right, to_left = first_pass(pack)
        go_right, go_left = second_pass(pack)
        to_right.wait_recv()
        pair_mid[pack, 0] = (
            pair_in[pack, 0, :, pl.ds(HALF, HALF), :] + power[slots, pl.ds(right_rows, HALF), :]
        )
        go_right.start()
        to_left.wait_recv()
        pair_mid[pack, 1] = (
            pair_in[pack, 1, :, pl.ds(0, HALF), :]
            + power[slots, pl.ds(pl.multiple_of(left_rows + HALF, 8), HALF), :]
        )
        go_left.start()

    def make_factor(pack):
        for copy in second_pass(pack):
            copy.wait_recv()
        for inner in range(PACK):
            slot = pack * PACK + inner
            own = power[slot, pl.ds(own_rows, QUARTER), :]
            top = own[:HALF] + pair_sum[pack, 0, inner] + pair_in[pack, 1, inner, pl.ds(HALF, HALF), :]
            bottom = own[HALF:] + pair_sum[pack, 1, inner] + pair_in[pack, 0, inner, pl.ds(0, HALF), :]
            intensity = jnp.concatenate([top, bottom], axis=0)
            ratio = 1.0 - amps[slot] * lax.rsqrt(jnp.maximum(intensity, 1.0))
            factor[slot, pl.ds(own_rows, QUARTER), :] = jnp.where(slot < counts[0], ratio, 0.0)
        for copy in third_pass(pack):
            copy.start()

    def relay_factor(pack):
        from_left, from_right = third_pass(pack, left_rows, right_rows)
        go_right, go_left = fourth_pass(pack)
        from_left.wait_recv()
        go_right.start()
        from_right.wait_recv()
        go_left.start()

    def backward(slot):
        scale = factor[slot]
        wave = far[slot]
        wide = jnp.concatenate([wave[:SIDE] * scale, wave[SIDE:] * scale], axis=1)
        back = both_sides(wide, table[2], table[3], table[0], table[1])
        back_re, back_im = back[:SIDE], back[SIDE:]
        probe_re, probe_im = probes[slot, 0], probes[slot, 1]
        shift = place_of(slot)[2]
        grads = (
            probe_re * back_re + probe_im * back_im,
            probe_re * back_im - probe_im * back_re,
        )
        for plane in range(2):
            turned = pltpu.roll(grads[plane], shift & (SIDE - 1), 1)
            placed[plane, 2 * slot, pl.ds(SIDE, SIDE), :] = jnp.where(lane >= shift, turned, 0.0)
            placed[plane, 2 * slot + 1, pl.ds(SIDE, SIDE), :] = jnp.where(lane < shift, turned, 0.0)
        patch_re, patch_im = patches[slot, 0], patches[slot, 1]
        pieces = (
            patch_re * back_re + patch_im * back_im,
            patch_re * back_im - patch_im * back_re,
        )
        for at in range(COMP):
            for plane in range(2):
                where_at = pl.ds((2 * at + plane) * SIDE, SIDE)
                terms[where_at, :] = terms[where_at, :] + weights[at, slot] * pieces[plane]

    def use_factor(pack):
        facing = pl.multiple_of(QUARTER * lax.rem(mode + 2, MODES), 8)
        for copy in fourth_pass(pack, facing, facing):
            copy.wait_recv()
        for inner in range(PACK):
            backward(pack * PACK + inner)

    stages = (send_power, relay_power, make_factor, relay_factor, use_factor)

    def step(at, carry):
        for place, stage in enumerate(stages):
            lag = place * LAG

            @pl.when((at >= lag) & (at < PACKS + lag))
            def _():
                stage(at - lag)

        return carry

    lax.fori_loop(0, PACKS + (len(stages) - 1) * LAG, step, 0)

    def gathered(plane, tile_at, start):
        total = None
        for slot in range(SLOTS):
            row, base, shift = place_of(slot)
            index = jnp.where(
                tile_at == base, 2 * slot, jnp.where(tile_at == base + 1, 2 * slot + 1, EMPTY)
            )
            value = placed[plane, index, pl.ds(start - row, SIDE), :]
            total = value if total is None else total + value
        return total

    order = ((2, 0), (2, 1), (1, 1), (3, 0), (1, 0), (3, 1), (0, 0), (0, 1))

    def block_of(at):
        turn, plane = order[at]
        return lax.rem(mode + turn, MODES), plane

    def chunk_rows(at):
        return pl.ds(pl.multiple_of(at * rows, 8), rows)

    def half_of(ref, at):
        return ref.at[pl.ds(pl.multiple_of(at * half_rows, 8), half_rows)]

    halves = send(half_of(terms, 1 - core), half_in, pair_sems.at[:, 0], {"tile": sibling})
    halves.start()

    rims = []

    def send_rims(start, stop):
        for at in range(start, stop):
            block, plane = block_of(at)
            for half in range(2):
                rim_out[at, half] = gathered(plane, 2 * block + half, 2 * SIDE)
            copy = send(rim_out.at[at], rim_in.at[at], rim_sems.at[:, at], {"tile": below})
            copy.start()
            rims.append(copy)

    send_rims(0, 2)
    halves.wait_recv()
    half_sum[...] = terms[pl.ds(pl.multiple_of(core * half_rows, 8), half_rows), :] + half_in[...]
    spread = []
    for step in range(1, across):
        copy = send(
            half_sum.at[chunk_rows(lax.rem(chip + step, across))],
            near_buf.at[step],
            near_sems.at[:, step],
            {"tile": near(step)},
        )
        copy.start()
        spread.append(copy)
    send_rims(2, 8)

    part_peers = ({"mode": right}, {"mode": left})
    part_kind = (0, 2, 1, 3, 4, 5)
    part_side = (0, 1, 0, 1, 0, 1)
    parts = [
        send(
            part.at[at],
            part_in.at[part_kind[at]],
            part_sems.at[:, part_kind[at]],
            part_peers[part_side[at]],
        )
        for at in range(6)
    ]
    arrivals = {part_kind[at]: parts[at] for at in range(6)}

    def whole(at, extra):
        block, plane = block_of(at)
        rims[at].wait_recv()
        for kind in extra:
            arrivals[kind].wait_recv()
        for half in range(2):
            value = gathered(plane, 2 * block + half, SIDE)
            value = value + jnp.where(tile > 0, rim_in[at, half], 0.0)
            for kind in extra:
                value = value + part_in[kind, half]
            yield half, value

    def to_owner(step):
        target = lax.rem(level + step, depth)
        at = pl.ds(pl.multiple_of(lax.rem(target, owners) * piece, 8), piece)
        return target, send(
            chunk.at[at], far_buf.at[step], far_sems.at[:, step], {"tile": beyond(step)}
        )

    def from_owner(source, step):
        at = pl.ds(pl.multiple_of(place * rows + lax.rem(source, owners) * piece, 8), piece)
        return send(
            probe_out.at[at], probe_out.at[at], back_sems.at[:, step], {"tile": beyond(step)}
        )

    for at in range(0, 2):
        for half, value in whole(at, ()):
            part[at, half] = value
        parts[at].start()

    for copy in spread:
        copy.wait_recv()
    total = half_sum[chunk_rows(chip), :]
    for step in range(1, across):
        total = total + near_buf[step]
    chunk[...] = total

    for step in range(1, depth):
        target, copy = to_owner(step)

        @pl.when(target < owners)
        def _():
            copy.start()

    for at in range(2, 4):
        for half, value in whole(at, ()):
            part[at, half] = value
        parts[at].start()

    @pl.when(level < owners)
    def _():
        for step in range(1, depth):
            to_owner(step)[1].wait_recv()
        total = chunk[pl.ds(pl.multiple_of(lax.rem(level, owners) * piece, 8), piece), :]
        for step in range(1, depth):
            total = total + far_buf[step]
        at = pl.ds(pl.multiple_of(place * rows + lax.rem(level, owners) * piece, 8), piece)
        probe_out[at, :] = total
        for step in range(1, depth):
            from_owner(level, step).start()

    for at in range(4, 6):
        for half, value in whole(at, (2 * (at - 4),)):
            part[at, half] = value
        parts[at].start()

    for step in range(1, depth):
        source = lax.rem(level - step + depth, depth)

        @pl.when(source < owners)
        def _():
            from_owner(source, step).wait_recv()

    def shared(source, step):
        at = chunk_rows(source)
        return send(
            probe_out.at[at], probe_out.at[at], spread_sems.at[:, step], {"tile": near(step)}
        )

    for step in range(1, across):
        shared(place, step).start()

    for at in range(6, 7):
        for half, value in whole(at, (4, 3) if at == 6 else (5, 1)):
            object_out[at - 6, :, pl.ds(half * SIDE, SIDE)] = value

    for step in range(1, across):
        shared(core * across + lax.rem(chip - step + across, across), step).wait_recv()

    def final(at):
        ref = half_of(probe_out, at)
        return send(ref, ref, pair_sems.at[:, 1], {"tile": sibling})

    final(core).start()
    for at in range(7, 8):
        for half, value in whole(at, (4, 3) if at == 6 else (5, 1)):
            object_out[at - 6, :, pl.ds(half * SIDE, SIDE)] = value
    final(1 - core).wait_recv()
    final(core).wait_send()
    halves.wait_send()
    for copy in halo + rims + parts + spread:
        copy.wait_send()
    for step in range(1, across):
        shared(place, step).wait_send()
    for step in range(1, depth):
        target, copy = to_owner(step)

        @pl.when(target < owners)
        def _():
            copy.wait_send()

    @pl.when(level < owners)
    def _():
        for step in range(1, depth):
            from_owner(level, step).wait_send()

    def settle(pack, carry):
        for make in (first_pass, second_pass, third_pass, fourth_pass):
            for copy in make(pack):
                copy.wait_send()
        return carry

    lax.fori_loop(0, PACKS, settle, 0)


def tables():
    line = np.arange(SIDE)
    angle = (line[:, None] * line[None, :] % SIDE) * (2.0 * math.pi / SIDE)
    cos = np.cos(angle) / math.sqrt(SIDE)
    sin = -np.sin(angle) / math.sqrt(SIDE)
    return np.stack([cos, sin]).astype(np.float32)


def local(object_field, components, relax_weights, amplitudes, positions, counts):
    tiles = lax.axis_size("tile")
    group = group_size(tiles)
    depth = tiles // group
    rows = COMP * 2 * SIDE // group
    piece = rows // owner_count(depth)
    f32 = jnp.float32
    anywhere = pl.BlockSpec(memory_space=pltpu.HBM)
    vector = pl.BlockSpec(memory_space=pltpu.VMEM)
    flops = 2 * 2 * SLOTS * 3 * 2 * 256 * 256 * 128
    object_grad, probe_grad = pl.pallas_call(
        functools.partial(kernel, tiles),
        out_shape=(
            jax.ShapeDtypeStruct((2, SIDE, 2 * SIDE), f32),
            jax.ShapeDtypeStruct((COMP * 2 * SIDE, SIDE), f32),
        ),
        in_specs=[anywhere] * 7,
        out_specs=(vector, vector),
        scratch_shapes=[
            pltpu.SMEM((COMP, SLOTS), f32),
            pltpu.SMEM((2, SLOTS), jnp.int32),
            pltpu.SMEM((1,), jnp.int32),
            pltpu.VMEM((4, 2 * SIDE, 2 * SIDE), jnp.bfloat16),
            pltpu.VMEM((2, SIDE, SIDE), f32),
            pltpu.VMEM((2, TILES_WIDE, 2 * SIDE, SIDE), f32),
            pltpu.VMEM((COMP, 2, SIDE, SIDE), f32),
            pltpu.VMEM((SLOTS, QUARTER, SIDE), f32),
            pltpu.VMEM((SLOTS, 2, SIDE, SIDE), f32),
            pltpu.VMEM((SLOTS, 2, SIDE, SIDE), f32),
            pltpu.VMEM((SLOTS, 2 * SIDE, SIDE), f32),
            pltpu.VMEM((SLOTS, SIDE + HALF, SIDE), f32),
            pltpu.VMEM((PACKS, 2, PACK, QUARTER, SIDE), f32),
            pltpu.VMEM((PACKS, 2, PACK, HALF, SIDE), f32),
            pltpu.VMEM((PACKS, 2, PACK, HALF, SIDE), f32),
            pltpu.VMEM((SLOTS, SIDE, SIDE), f32),
            pltpu.VMEM((2, EMPTY + 1, 3 * SIDE, SIDE), f32),
            pltpu.VMEM((8, 2, SIDE, SIDE), f32),
            pltpu.VMEM((8, 2, SIDE, SIDE), f32),
            pltpu.VMEM((6, 2, SIDE, SIDE), f32),
            pltpu.VMEM((6, 2, SIDE, SIDE), f32),
            pltpu.VMEM((COMP * 2 * SIDE, SIDE), f32),
            pltpu.VMEM((COMP * SIDE, SIDE), f32),
            pltpu.VMEM((COMP * SIDE, SIDE), f32),
            pltpu.VMEM((rows, SIDE), f32),
            pltpu.VMEM((group // 2, rows, SIDE), f32),
            pltpu.VMEM((depth, piece, SIDE), f32),
            pltpu.SemaphoreType.DMA((6 + TILES_WIDE,)),
            pltpu.SemaphoreType.DMA((2, TILES_WIDE)),
            pltpu.SemaphoreType.DMA((2, PACKS, 8)),
            pltpu.SemaphoreType.DMA((2, 8)),
            pltpu.SemaphoreType.DMA((2, 6)),
            pltpu.SemaphoreType.DMA((2, 2)),
            pltpu.SemaphoreType.DMA((2, group // 2)),
            pltpu.SemaphoreType.DMA((2, depth)),
            pltpu.SemaphoreType.DMA((2, depth)),
            pltpu.SemaphoreType.DMA((2, group // 2)),
        ],
        compiler_params=pltpu.CompilerParams(
            collective_id=0, has_side_effects=True, vmem_limit_bytes=62 * 1024 * 1024
        ),
        cost_estimate=pl.CostEstimate(
            flops=flops, bytes_accessed=4 * 1024 * 1024, transcendentals=SLOTS * SIDE * SIDE
        ),
    )(
        object_field,
        components,
        relax_weights.T,
        amplitudes,
        positions.T,
        counts,
        jnp.asarray(tables()),
    )
    return object_grad, probe_grad.reshape(1, COMP, 2, SIDE, SIDE)


def solution(mesh):
    return jax.shard_map(
        local,
        mesh=mesh,
        in_specs=(
            P(None, "tile", None),
            P("mode", None, None, None, None),
            P("tile", None),
            P("tile", None, None),
            P("tile", None),
            P("tile"),
        ),
        out_specs=(P(None, "tile", "mode"), P("mode", None, None, None, None)),
        check_vma=False,
    )
```

```python
import functools
import math

import jax
import jax.numpy as jnp
import numpy as np
from jax import lax
from jax.experimental import pallas as pl
from jax.experimental.pallas import tpu as pltpu
from jax.sharding import PartitionSpec as P

MESH = pl.DeviceIdType.MESH
SIDE = 128
SLOTS = 8
COMP = 4
MODES = 4
TILES_WIDE = 8
QUARTER = 32
HALF = 16
EMPTY = 2 * SLOTS
PACK = 2
PACKS = SLOTS // PACK
LAGS = (0, 3, 6, 9, 12)


def group_size(tiles):
    return 8 if tiles % 16 == 0 else 4


def owner_count(depth):
    return 1 << (depth.bit_length() - 1)


def split(values):
    high = values.astype(jnp.bfloat16)
    low = (values - high.astype(jnp.float32)).astype(jnp.bfloat16)
    return high, low


def dot(left, right):
    return jnp.dot(left, right, preferred_element_type=jnp.float32)


def both_sides(wide, right_high, right_low, left_high, left_low):
    high, low = split(wide)
    middle = dot(high, right_high) + dot(low, right_high) + dot(high, right_low)
    count = wide.shape[0] // SIDE
    blocks = [middle[at * SIDE : (at + 1) * SIDE] for at in range(count)]
    columns = [jnp.concatenate([block[:, :SIDE], block[:, SIDE:]], axis=0) for block in blocks]
    tall = jnp.concatenate(columns, axis=1)
    high, low = split(tall)
    return dot(left_high, high) + dot(left_high, low) + dot(left_low, high)


def kernel(
    tiles,
    object_ref,
    components_ref,
    weights_ref,
    amplitudes_ref,
    positions_ref,
    counts_ref,
    table_ref,
    object_out,
    probe_out,
    weights,
    positions,
    counts,
    table,
    waves,
    ext,
    comp,
    amps,
    patches,
    probes,
    far,
    power,
    pair_in,
    pair_mid,
    pair_sum,
    factor,
    placed,
    rim_out,
    rim_in,
    part,
    part_in,
    terms,
    half_in,
    half_sum,
    chunk,
    near_buf,
    far_buf,
    local_sems,
    halo_sems,
    slot_sems,
    rim_sems,
    part_sems,
    pair_sems,
    near_sems,
    far_sems,
    back_sems,
    spread_sems,
):
    group = group_size(tiles)
    depth = tiles // group
    owners = owner_count(depth)
    rows = COMP * 2 * SIDE // group
    piece = rows // owners
    tile = lax.axis_index("tile")
    mode = lax.axis_index("mode")
    above = lax.rem(tile + tiles - 1, tiles)
    below = lax.rem(tile + 1, tiles)
    right = lax.rem(mode + 1, MODES)
    left = lax.rem(mode + MODES - 1, MODES)
    mine = lax.rem(tile, group)
    level = lax.div(tile, group)

    across = group // 2
    core = lax.rem(mine, 2)
    chip = lax.div(mine, 2)
    place = core * across + chip
    sibling = level * group + chip * 2 + 1 - core
    half_rows = COMP * SIDE

    def near(step):
        return level * group + lax.rem(chip + step, across) * 2 + core

    def beyond(step):
        return lax.rem(level + step, depth) * group + mine

    def send(src, dst, sems, peer):
        return pltpu.make_async_remote_copy(
            src_ref=src,
            dst_ref=dst,
            send_sem=sems.at[0],
            recv_sem=sems.at[1],
            device_id=peer,
            device_id_type=MESH,
        )

    def columns(ref, at):
        return ref.at[:, :, pl.ds(at * SIDE, SIDE)]

    barrier = pltpu.get_barrier_semaphore()
    peers = [{"tile": above}, {"tile": below}, {"mode": right}, {"mode": left}]
    peers += [{"tile": sibling}]
    peers += [{"tile": near(step)} for step in range(1, across)]
    peers += [{"tile": beyond(step)} for step in range(1, depth)]
    for peer in peers:
        pl.semaphore_signal(barrier, inc=1, device_id=peer, device_id_type=MESH)
    loads = [
        pltpu.make_async_copy(weights_ref, weights, local_sems.at[10]),
        pltpu.make_async_copy(positions_ref, positions, local_sems.at[11]),
        pltpu.make_async_copy(counts_ref, counts, local_sems.at[12]),
        pltpu.make_async_copy(table_ref, waves, local_sems.at[13]),
        pltpu.make_async_copy(components_ref.at[0], comp, local_sems.at[0]),
        pltpu.make_async_copy(
            amplitudes_ref.at[:, pl.ds(pl.multiple_of(mode * QUARTER, 8), QUARTER), :],
            amps,
            local_sems.at[1],
        ),
    ] + [
        pltpu.make_async_copy(
            columns(object_ref, at), ext.at[:, at, pl.ds(0, SIDE), :], local_sems.at[2 + at]
        )
        for at in range(TILES_WIDE)
    ]
    for copy in loads:
        copy.start()
    pl.semaphore_wait(barrier, len(peers))

    halo = [
        send(
            columns(object_ref, at),
            ext.at[:, at, pl.ds(SIDE, SIDE), :],
            halo_sems.at[:, at],
            {"tile": above},
        )
        for at in range(TILES_WIDE)
    ]
    for copy in halo:
        copy.start()

    terms[...] = jnp.zeros_like(terms)

    def clear(at, carry):
        for plane in range(2):
            placed[plane, at, pl.ds(0, SIDE), :] = jnp.zeros((SIDE, SIDE), jnp.float32)
            placed[plane, at, pl.ds(2 * SIDE, SIDE), :] = jnp.zeros((SIDE, SIDE), jnp.float32)
        return carry

    lax.fori_loop(0, EMPTY + 1, clear, 0)
    for plane in range(2):
        placed[plane, EMPTY, pl.ds(SIDE, SIDE), :] = jnp.zeros((SIDE, SIDE), jnp.float32)
    for copy in loads:
        copy.wait()
    cos_high, cos_low = split(waves[0])
    sin_high, sin_low = split(waves[1])
    for at, (cos, sin) in enumerate(((cos_high, sin_high), (cos_low, sin_low))):
        lower = jnp.concatenate([-sin, cos], axis=1)
        upper = jnp.concatenate([cos, sin], axis=1)
        table[at] = jnp.concatenate([upper, lower], axis=0)
        lower = jnp.concatenate([sin, cos], axis=1)
        upper = jnp.concatenate([cos, -sin], axis=1)
        table[2 + at] = jnp.concatenate([upper, lower], axis=0)

    def mix(slot, carry):
        for plane in range(2):
            total = weights[0, slot] * comp[0, plane]
            for at in range(1, COMP):
                total = total + weights[at, slot] * comp[at, plane]
            probes[slot, plane] = total
        return carry

    lax.fori_loop(0, SLOTS, mix, 0)
    for copy in halo:
        copy.wait_recv()

    @pl.when(tile == tiles - 1)
    def _():
        for plane in range(2):
            for at in range(TILES_WIDE):
                ext[plane, at, pl.ds(SIDE, SIDE), :] = jnp.zeros((SIDE, SIDE), jnp.float32)

    lane = lax.broadcasted_iota(jnp.int32, (SIDE, SIDE), 1)

    def place_of(slot):
        row = positions[0, slot] & (SIDE - 1)
        col = positions[1, slot]
        base = jnp.minimum(lax.shift_right_logical(col, 7), TILES_WIDE - 2)
        return row, base, col - base * SIDE

    def take(slot, plane):
        row, base, shift = place_of(slot)
        turn = (SIDE - shift) & (SIDE - 1)
        first = pltpu.roll(ext[plane, base, pl.ds(row, SIDE), :], turn, 1)
        second = pltpu.roll(ext[plane, base + 1, pl.ds(row, SIDE), :], turn, 1)
        return jnp.where(lane < SIDE - shift, first, second)

    ahead = pl.multiple_of(lax.rem(QUARTER * (mode + 1) + HALF, SIDE), 8)
    behind = pl.multiple_of(lax.rem(QUARTER * (mode + 2) + HALF, SIDE), 8)
    own_rows = pl.multiple_of(QUARTER * mode, 8)
    right_rows = pl.multiple_of(QUARTER * right, 8)
    left_rows = pl.multiple_of(QUARTER * left, 8)

    def slots_of(pack):
        return pl.ds(pack * PACK, PACK)

    def first_pass(pack):
        return [
            send(
                power.at[slots_of(pack), pl.ds(ahead, QUARTER), :],
                pair_in.at[pack, 0],
                slot_sems.at[:, pack, 0],
                {"mode": right},
            ),
            send(
                power.at[slots_of(pack), pl.ds(behind, QUARTER), :],
                pair_in.at[pack, 1],
                slot_sems.at[:, pack, 1],
                {"mode": left},
            ),
        ]

    def second_pass(pack):
        return [
            send(
                pair_mid.at[pack, 0],
                pair_sum.at[pack, 0],
                slot_sems.at[:, pack, 2],
                {"mode": right},
            ),
            send(
                pair_mid.at[pack, 1],
                pair_sum.at[pack, 1],
                slot_sems.at[:, pack, 3],
                {"mode": left},
            ),
        ]

    def in_place(pack, start, count, kind, peer):
        ref = factor.at[slots_of(pack), pl.ds(start, count), :]
        return send(ref, ref, slot_sems.at[:, pack, kind], {"mode": peer})

    def third_pass(pack, start_right=own_rows, start_left=own_rows):
        return [
            in_place(pack, start_right, QUARTER, 4, right),
            in_place(pack, start_left, QUARTER, 5, left),
        ]

    def fourth_pass(pack, top=left_rows, bottom=right_rows):
        return [
            in_place(pack, top, HALF, 6, right),
            in_place(pack, pl.multiple_of(bottom + HALF, 8), HALF, 7, left),
        ]

    def exit_wave(slot):
        for plane in range(2):
            patches[slot, plane] = take(slot, plane)
        probe_re, probe_im = probes[slot, 0], probes[slot, 1]
        patch_re, patch_im = patches[slot, 0], patches[slot, 1]
        return jnp.concatenate(
            [
                probe_re * patch_re - probe_im * patch_im,
                probe_re * patch_im + probe_im * patch_re,
            ],
            axis=1,
        )

    def forward(pack):
        slots = [pack * PACK + inner for inner in range(PACK)]
        wide = jnp.concatenate([exit_wave(slot) for slot in slots], axis=0)
        waves_out = both_sides(wide, table[0], table[1], table[2], table[3])
        for inner, slot in enumerate(slots):
            wave = waves_out[:, inner * SIDE : (inner + 1) * SIDE]
            far[slot] = wave
            strength = wave[:SIDE] * wave[:SIDE] + wave[SIDE:] * wave[SIDE:]
            power[slot, pl.ds(0, SIDE), :] = strength
            power[slot, pl.ds(SIDE, HALF), :] = strength[:HALF]

    def send_power(pack):
        forward(pack)
        for copy in first_pass(pack):
            copy.start()

    def relay_power(pack):
        slots = slots_of(pack)
        to_right, to_left = first_pass(pack)
        go_right, go_left = second_pass(pack)
        to_right.wait_recv()
        pair_mid[pack, 0] = (
            pair_in[pack, 0, :, pl.ds(HALF, HALF), :] + power[slots, pl.ds(right_rows, HALF), :]
        )
        go_right.start()
        to_left.wait_recv()
        pair_mid[pack, 1] = (
            pair_in[pack, 1, :, pl.ds(0, HALF), :]
            + power[slots, pl.ds(pl.multiple_of(left_rows + HALF, 8), HALF), :]
        )
        go_left.start()

    def make_factor(pack):
        for copy in second_pass(pack):
            copy.wait_recv()
        for inner in range(PACK):
            slot = pack * PACK + inner
            own = power[slot, pl.ds(own_rows, QUARTER), :]
            top = own[:HALF] + pair_sum[pack, 0, inner] + pair_in[pack, 1, inner, pl.ds(HALF, HALF), :]
            bottom = own[HALF:] + pair_sum[pack, 1, inner] + pair_in[pack, 0, inner, pl.ds(0, HALF), :]
            intensity = jnp.concatenate([top, bottom], axis=0)
            ratio = 1.0 - amps[slot] * lax.rsqrt(jnp.maximum(intensity, 1.0))
            factor[slot, pl.ds(own_rows, QUARTER), :] = jnp.where(slot < counts[0], ratio, 0.0)
        for copy in third_pass(pack):
            copy.start()

    def relay_factor(pack):
        from_left, from_right = third_pass(pack, left_rows, right_rows)
        go_right, go_left = fourth_pass(pack)
        from_left.wait_recv()
        go_right.start()
        from_right.wait_recv()
        go_left.start()

    def residue(slot):
        scale = factor[slot]
        wave = far[slot]
        return jnp.concatenate([wave[:SIDE] * scale, wave[SIDE:] * scale], axis=1)

    def backward(pack):
        slots = [pack * PACK + inner for inner in range(PACK)]
        wide = jnp.concatenate([residue(slot) for slot in slots], axis=0)
        backs = both_sides(wide, table[2], table[3], table[0], table[1])
        for inner, slot in enumerate(slots):
            add_gradients(slot, backs[:, inner * SIDE : (inner + 1) * SIDE])

    def add_gradients(slot, back):
        back_re, back_im = back[:SIDE], back[SIDE:]
        probe_re, probe_im = probes[slot, 0], probes[slot, 1]
        shift = place_of(slot)[2]
        grads = (
            probe_re * back_re + probe_im * back_im,
            probe_re * back_im - probe_im * back_re,
        )
        for plane in range(2):
            turned = pltpu.roll(grads[plane], shift & (SIDE - 1), 1)
            placed[plane, 2 * slot, pl.ds(SIDE, SIDE), :] = jnp.where(lane >= shift, turned, 0.0)
            placed[plane, 2 * slot + 1, pl.ds(SIDE, SIDE), :] = jnp.where(lane < shift, turned, 0.0)
        patch_re, patch_im = patches[slot, 0], patches[slot, 1]
        pieces = (
            patch_re * back_re + patch_im * back_im,
            patch_re * back_im - patch_im * back_re,
        )
        for at in range(COMP):
            for plane in range(2):
                where_at = pl.ds((2 * at + plane) * SIDE, SIDE)
                terms[where_at, :] = terms[where_at, :] + weights[at, slot] * pieces[plane]

    def use_factor(pack):
        facing = pl.multiple_of(QUARTER * lax.rem(mode + 2, MODES), 8)
        for copy in fourth_pass(pack, facing, facing):
            copy.wait_recv()
        backward(pack)

    stages = (send_power, relay_power, make_factor, relay_factor, use_factor)

    def step(at, carry):
        for place, stage in enumerate(stages):
            lag = LAGS[place]

            @pl.when((at >= lag) & (at < PACKS + lag))
            def _():
                stage(at - lag)

        return carry

    lax.fori_loop(0, PACKS + LAGS[-1], step, 0)

    def gathered(plane, tile_at, start):
        total = None
        for slot in range(SLOTS):
            row, base, shift = place_of(slot)
            index = jnp.where(
                tile_at == base, 2 * slot, jnp.where(tile_at == base + 1, 2 * slot + 1, EMPTY)
            )
            value = placed[plane, index, pl.ds(start - row, SIDE), :]
            total = value if total is None else total + value
        return total

    order = ((2, 0), (2, 1), (1, 1), (3, 0), (1, 0), (3, 1), (0, 0), (0, 1))

    def block_of(at):
        turn, plane = order[at]
        return lax.rem(mode + turn, MODES), plane

    def chunk_rows(at):
        return pl.ds(pl.multiple_of(at * rows, 8), rows)

    def half_of(ref, at):
        return ref.at[pl.ds(pl.multiple_of(at * half_rows, 8), half_rows)]

    halves = send(half_of(terms, 1 - core), half_in, pair_sems.at[:, 0], {"tile": sibling})
    halves.start()

    rims = []

    def send_rims(start, stop):
        for at in range(start, stop):
            block, plane = block_of(at)
            for half in range(2):
                rim_out[at, half] = gathered(plane, 2 * block + half, 2 * SIDE)
                copy = send(
                    rim_out.at[at, half],
                    rim_in.at[at, half],
                    rim_sems.at[:, at, half],
                    {"tile": below},
                )
                copy.start()
                rims.append(copy)

    send_rims(0, 2)
    halves.wait_recv()
    half_sum[...] = terms[pl.ds(pl.multiple_of(core * half_rows, 8), half_rows), :] + half_in[...]
    spread = []
    for step in range(1, across):
        copy = send(
            half_sum.at[chunk_rows(lax.rem(chip + step, across))],
            near_buf.at[step],
            near_sems.at[:, step],
            {"tile": near(step)},
        )
        copy.start()
        spread.append(copy)
    send_rims(2, 8)

    part_peers = ({"mode": right}, {"mode": left})
    part_kind = (0, 2, 1, 3, 4, 5)
    part_side = (0, 1, 0, 1, 0, 1)
    parts = [
        send(
            part.at[at, half],
            part_in.at[part_kind[at], half],
            part_sems.at[:, part_kind[at], half],
            part_peers[part_side[at]],
        )
        for at in range(6)
        for half in range(2)
    ]
    arrivals = {part_kind[at]: parts[2 * at : 2 * at + 2] for at in range(6)}

    def whole(at, extra):
        block, plane = block_of(at)
        for half in range(2):
            rims[2 * at + half].wait_recv()
            for kind in extra:
                arrivals[kind][half].wait_recv()
            value = gathered(plane, 2 * block + half, SIDE)
            value = value + jnp.where(tile > 0, rim_in[at, half], 0.0)
            for kind in extra:
                value = value + part_in[kind, half]
            yield half, value

    def to_owner(step):
        target = lax.rem(level + step, depth)
        at = pl.ds(pl.multiple_of(lax.rem(target, owners) * piece, 8), piece)
        return target, send(
            chunk.at[at], far_buf.at[step], far_sems.at[:, step], {"tile": beyond(step)}
        )

    def from_owner(source, step):
        at = pl.ds(pl.multiple_of(place * rows + lax.rem(source, owners) * piece, 8), piece)
        return send(
            probe_out.at[at], probe_out.at[at], back_sems.at[:, step], {"tile": beyond(step)}
        )

    for at in range(0, 2):
        for half, value in whole(at, ()):
            part[at, half] = value
            parts[2 * at + half].start()

    for copy in spread:
        copy.wait_recv()
    total = half_sum[chunk_rows(chip), :]
    for step in range(1, across):
        total = total + near_buf[step]
    chunk[...] = total

    for step in range(1, depth):
        target, copy = to_owner(step)

        @pl.when(target < owners)
        def _():
            copy.start()

    for at in range(2, 4):
        for half, value in whole(at, ()):
            part[at, half] = value
            parts[2 * at + half].start()

    @pl.when(level < owners)
    def _():
        for step in range(1, depth):
            to_owner(step)[1].wait_recv()
        total = chunk[pl.ds(pl.multiple_of(lax.rem(level, owners) * piece, 8), piece), :]
        for step in range(1, depth):
            total = total + far_buf[step]
        at = pl.ds(pl.multiple_of(place * rows + lax.rem(level, owners) * piece, 8), piece)
        probe_out[at, :] = total
        for step in range(1, depth):
            from_owner(level, step).start()

    for at in range(4, 6):
        for half, value in whole(at, (2 * (at - 4),)):
            part[at, half] = value
            parts[2 * at + half].start()

    for step in range(1, depth):
        source = lax.rem(level - step + depth, depth)

        @pl.when(source < owners)
        def _():
            from_owner(source, step).wait_recv()

    def shared(source, step):
        at = chunk_rows(source)
        return send(
            probe_out.at[at], probe_out.at[at], spread_sems.at[:, step], {"tile": near(step)}
        )

    for step in range(1, across):
        shared(place, step).start()

    for step in range(1, across):
        shared(core * across + lax.rem(chip - step + across, across), step).wait_recv()

    def final(at):
        ref = half_of(probe_out, at)
        return send(ref, ref, pair_sems.at[:, 1], {"tile": sibling})

    final(core).start()
    for at in range(6, 8):
        for half, value in whole(at, (4, 3) if at == 6 else (5, 1)):
            object_out[at - 6, :, pl.ds(half * SIDE, SIDE)] = value
    final(1 - core).wait_recv()
    final(core).wait_send()
    halves.wait_send()
    for copy in halo + rims + parts + spread:
        copy.wait_send()
    for step in range(1, across):
        shared(place, step).wait_send()
    for step in range(1, depth):
        target, copy = to_owner(step)

        @pl.when(target < owners)
        def _():
            copy.wait_send()

    @pl.when(level < owners)
    def _():
        for step in range(1, depth):
            from_owner(level, step).wait_send()

    def settle(pack, carry):
        for make in (first_pass, second_pass, third_pass, fourth_pass):
            for copy in make(pack):
                copy.wait_send()
        return carry

    lax.fori_loop(0, PACKS, settle, 0)


def tables():
    line = np.arange(SIDE)
    angle = (line[:, None] * line[None, :] % SIDE) * (2.0 * math.pi / SIDE)
    cos = np.cos(angle) / math.sqrt(SIDE)
    sin = -np.sin(angle) / math.sqrt(SIDE)
    return np.stack([cos, sin]).astype(np.float32)


def local(object_field, components, relax_weights, amplitudes, positions, counts):
    tiles = lax.axis_size("tile")
    group = group_size(tiles)
    depth = tiles // group
    rows = COMP * 2 * SIDE // group
    piece = rows // owner_count(depth)
    f32 = jnp.float32
    anywhere = pl.BlockSpec(memory_space=pltpu.HBM)
    vector = pl.BlockSpec(memory_space=pltpu.VMEM)
    flops = 2 * 2 * SLOTS * 3 * 2 * 256 * 256 * 128
    object_grad, probe_grad = pl.pallas_call(
        functools.partial(kernel, tiles),
        out_shape=(
            jax.ShapeDtypeStruct((2, SIDE, 2 * SIDE), f32),
            jax.ShapeDtypeStruct((COMP * 2 * SIDE, SIDE), f32),
        ),
        in_specs=[anywhere] * 7,
        out_specs=(vector, vector),
        scratch_shapes=[
            pltpu.SMEM((COMP, SLOTS), f32),
            pltpu.SMEM((2, SLOTS), jnp.int32),
            pltpu.SMEM((1,), jnp.int32),
            pltpu.VMEM((4, 2 * SIDE, 2 * SIDE), jnp.bfloat16),
            pltpu.VMEM((2, SIDE, SIDE), f32),
            pltpu.VMEM((2, TILES_WIDE, 2 * SIDE, SIDE), f32),
            pltpu.VMEM((COMP, 2, SIDE, SIDE), f32),
            pltpu.VMEM((SLOTS, QUARTER, SIDE), f32),
            pltpu.VMEM((SLOTS, 2, SIDE, SIDE), f32),
            pltpu.VMEM((SLOTS, 2, SIDE, SIDE), f32),
            pltpu.VMEM((SLOTS, 2 * SIDE, SIDE), f32),
            pltpu.VMEM((SLOTS, SIDE + HALF, SIDE), f32),
            pltpu.VMEM((PACKS, 2, PACK, QUARTER, SIDE), f32),
            pltpu.VMEM((PACKS, 2, PACK, HALF, SIDE), f32),
            pltpu.VMEM((PACKS, 2, PACK, HALF, SIDE), f32),
            pltpu.VMEM((SLOTS, SIDE, SIDE), f32),
            pltpu.VMEM((2, EMPTY + 1, 3 * SIDE, SIDE), f32),
            pltpu.VMEM((8, 2, SIDE, SIDE), f32),
            pltpu.VMEM((8, 2, SIDE, SIDE), f32),
            pltpu.VMEM((6, 2, SIDE, SIDE), f32),
            pltpu.VMEM((6, 2, SIDE, SIDE), f32),
            pltpu.VMEM((COMP * 2 * SIDE, SIDE), f32),
            pltpu.VMEM((COMP * SIDE, SIDE), f32),
            pltpu.VMEM((COMP * SIDE, SIDE), f32),
            pltpu.VMEM((rows, SIDE), f32),
            pltpu.VMEM((group // 2, rows, SIDE), f32),
            pltpu.VMEM((depth, piece, SIDE), f32),
            pltpu.SemaphoreType.DMA((6 + TILES_WIDE,)),
            pltpu.SemaphoreType.DMA((2, TILES_WIDE)),
            pltpu.SemaphoreType.DMA((2, PACKS, 8)),
            pltpu.SemaphoreType.DMA((2, 8, 2)),
            pltpu.SemaphoreType.DMA((2, 6, 2)),
            pltpu.SemaphoreType.DMA((2, 2)),
            pltpu.SemaphoreType.DMA((2, group // 2)),
            pltpu.SemaphoreType.DMA((2, depth)),
            pltpu.SemaphoreType.DMA((2, depth)),
            pltpu.SemaphoreType.DMA((2, group // 2)),
        ],
        compiler_params=pltpu.CompilerParams(
            collective_id=0, has_side_effects=True, vmem_limit_bytes=62 * 1024 * 1024
        ),
        cost_estimate=pl.CostEstimate(
            flops=flops, bytes_accessed=4 * 1024 * 1024, transcendentals=SLOTS * SIDE * SIDE
        ),
    )(
        object_field,
        components,
        relax_weights.T,
        amplitudes,
        positions.T,
        counts,
        jnp.asarray(tables()),
    )
    return object_grad, probe_grad.reshape(1, COMP, 2, SIDE, SIDE)


def solution(mesh):
    return jax.shard_map(
        local,
        mesh=mesh,
        in_specs=(
            P(None, "tile", None),
            P("mode", None, None, None, None),
            P("tile", None),
            P("tile", None, None),
            P("tile", None),
            P("tile"),
        ),
        out_specs=(P(None, "tile", "mode"), P("mode", None, None, None, None)),
        check_vma=False,
    )
```

```python
import functools
import math

import jax
import jax.numpy as jnp
import numpy as np
from jax import lax
from jax.experimental import pallas as pl
from jax.experimental.pallas import tpu as pltpu
from jax.sharding import PartitionSpec as P

MESH = pl.DeviceIdType.MESH
SIDE = 128
SLOTS = 8
COMP = 4
MODES = 4
TILES_WIDE = 8
QUARTER = 32
HALF = 16
EMPTY = 2 * SLOTS
PACK = 2
PACKS = SLOTS // PACK
LAGS = (0, 3, 6, 9, 12)


def group_size(tiles):
    return 8 if tiles % 16 == 0 else 4


def owner_count(depth):
    return 1 << (depth.bit_length() - 1)


def split(values):
    high = values.astype(jnp.bfloat16)
    low = (values - high.astype(jnp.float32)).astype(jnp.bfloat16)
    return high, low


def dot(left, right):
    return jnp.dot(left, right, preferred_element_type=jnp.float32)


def both_sides(wide, right_high, right_low, left_high, left_low):
    high, low = split(wide)
    middle = dot(high, right_high) + dot(low, right_high) + dot(high, right_low)
    count = wide.shape[0] // SIDE
    blocks = [middle[at * SIDE : (at + 1) * SIDE] for at in range(count)]
    columns = [jnp.concatenate([block[:, :SIDE], block[:, SIDE:]], axis=0) for block in blocks]
    tall = jnp.concatenate(columns, axis=1)
    high, low = split(tall)
    return dot(left_high, high) + dot(left_high, low) + dot(left_low, high)


def kernel(
    tiles,
    object_ref,
    components_ref,
    weights_ref,
    amplitudes_ref,
    positions_ref,
    counts_ref,
    table_ref,
    object_out,
    probe_out,
    weights,
    positions,
    counts,
    table,
    waves,
    ext,
    comp,
    amps,
    patches,
    probes,
    far,
    power,
    pair_in,
    pair_mid,
    pair_sum,
    factor,
    placed,
    rim_out,
    rim_in,
    part,
    part_in,
    terms,
    half_in,
    half_sum,
    chunk,
    near_buf,
    far_buf,
    local_sems,
    halo_sems,
    slot_sems,
    rim_sems,
    part_sems,
    pair_sems,
    near_sems,
    far_sems,
    back_sems,
    spread_sems,
):
    group = group_size(tiles)
    depth = tiles // group
    owners = owner_count(depth)
    rows = COMP * 2 * SIDE // group
    piece = rows // owners
    tile = lax.axis_index("tile")
    mode = lax.axis_index("mode")
    above = lax.rem(tile + tiles - 1, tiles)
    below = lax.rem(tile + 1, tiles)
    right = lax.rem(mode + 1, MODES)
    left = lax.rem(mode + MODES - 1, MODES)
    mine = lax.rem(tile, group)
    level = lax.div(tile, group)

    across = group // 2
    core = lax.rem(mine, 2)
    chip = lax.div(mine, 2)
    place = core * across + chip
    sibling = level * group + chip * 2 + 1 - core
    half_rows = COMP * SIDE

    def near(step):
        return level * group + lax.rem(chip + step, across) * 2 + core

    def beyond(step):
        return lax.rem(level + step, depth) * group + mine

    def send(src, dst, sems, peer):
        return pltpu.make_async_remote_copy(
            src_ref=src,
            dst_ref=dst,
            send_sem=sems.at[0],
            recv_sem=sems.at[1],
            device_id=peer,
            device_id_type=MESH,
        )

    def columns(ref, at):
        return ref.at[:, :, pl.ds(at * SIDE, SIDE)]

    barrier = pltpu.get_barrier_semaphore()
    peers = [{"tile": above}, {"tile": below}, {"mode": right}, {"mode": left}]
    peers += [{"tile": sibling}]
    peers += [{"tile": near(step)} for step in range(1, across)]
    peers += [{"tile": beyond(step)} for step in range(1, depth)]
    for peer in peers:
        pl.semaphore_signal(barrier, inc=1, device_id=peer, device_id_type=MESH)
    loads = [
        pltpu.make_async_copy(weights_ref, weights, local_sems.at[10]),
        pltpu.make_async_copy(positions_ref, positions, local_sems.at[11]),
        pltpu.make_async_copy(counts_ref, counts, local_sems.at[12]),
        pltpu.make_async_copy(table_ref, waves, local_sems.at[13]),
        pltpu.make_async_copy(components_ref.at[0], comp, local_sems.at[0]),
        pltpu.make_async_copy(
            amplitudes_ref.at[:, pl.ds(pl.multiple_of(mode * QUARTER, 8), QUARTER), :],
            amps,
            local_sems.at[1],
        ),
    ] + [
        pltpu.make_async_copy(
            columns(object_ref, at), ext.at[:, at, pl.ds(0, SIDE), :], local_sems.at[2 + at]
        )
        for at in range(TILES_WIDE)
    ]
    for copy in loads:
        copy.start()
    pl.semaphore_wait(barrier, len(peers))

    halo = [
        send(
            columns(object_ref, at),
            ext.at[:, at, pl.ds(SIDE, SIDE), :],
            halo_sems.at[:, at],
            {"tile": above},
        )
        for at in range(TILES_WIDE)
    ]
    for copy in halo:
        copy.start()

    terms[...] = jnp.zeros_like(terms)

    def clear(at, carry):
        for plane in range(2):
            placed[plane, at, pl.ds(0, SIDE), :] = jnp.zeros((SIDE, SIDE), jnp.float32)
            placed[plane, at, pl.ds(2 * SIDE, SIDE), :] = jnp.zeros((SIDE, SIDE), jnp.float32)
        return carry

    lax.fori_loop(0, EMPTY + 1, clear, 0)
    for plane in range(2):
        placed[plane, EMPTY, pl.ds(SIDE, SIDE), :] = jnp.zeros((SIDE, SIDE), jnp.float32)
    for copy in loads:
        copy.wait()
    cos_high, cos_low = split(waves[0])
    sin_high, sin_low = split(waves[1])
    for at, (cos, sin) in enumerate(((cos_high, sin_high), (cos_low, sin_low))):
        lower = jnp.concatenate([-sin, cos], axis=1)
        upper = jnp.concatenate([cos, sin], axis=1)
        table[at] = jnp.concatenate([upper, lower], axis=0)
        lower = jnp.concatenate([sin, cos], axis=1)
        upper = jnp.concatenate([cos, -sin], axis=1)
        table[2 + at] = jnp.concatenate([upper, lower], axis=0)

    def mix(slot, carry):
        for plane in range(2):
            total = weights[0, slot] * comp[0, plane]
            for at in range(1, COMP):
                total = total + weights[at, slot] * comp[at, plane]
            probes[slot, plane] = total
        return carry

    lax.fori_loop(0, SLOTS, mix, 0)
    for copy in halo:
        copy.wait_recv()

    @pl.when(tile == tiles - 1)
    def _():
        for plane in range(2):
            for at in range(TILES_WIDE):
                ext[plane, at, pl.ds(SIDE, SIDE), :] = jnp.zeros((SIDE, SIDE), jnp.float32)

    lane = lax.broadcasted_iota(jnp.int32, (SIDE, SIDE), 1)

    def place_of(slot):
        row = positions[0, slot] & (SIDE - 1)
        col = positions[1, slot]
        base = jnp.minimum(lax.shift_right_logical(col, 7), TILES_WIDE - 2)
        return row, base, col - base * SIDE

    def take(slot, plane):
        row, base, shift = place_of(slot)
        turn = (SIDE - shift) & (SIDE - 1)
        first = pltpu.roll(ext[plane, base, pl.ds(row, SIDE), :], turn, 1)
        second = pltpu.roll(ext[plane, base + 1, pl.ds(row, SIDE), :], turn, 1)
        return jnp.where(lane < SIDE - shift, first, second)

    ahead = pl.multiple_of(lax.rem(QUARTER * (mode + 1) + HALF, SIDE), 8)
    behind = pl.multiple_of(lax.rem(QUARTER * (mode + 2) + HALF, SIDE), 8)
    own_rows = pl.multiple_of(QUARTER * mode, 8)
    right_rows = pl.multiple_of(QUARTER * right, 8)
    left_rows = pl.multiple_of(QUARTER * left, 8)

    def slots_of(pack):
        return pl.ds(pack * PACK, PACK)

    def first_pass(pack):
        return [
            send(
                power.at[slots_of(pack), pl.ds(ahead, QUARTER), :],
                pair_in.at[pack, 0],
                slot_sems.at[:, pack, 0],
                {"mode": right},
            ),
            send(
                power.at[slots_of(pack), pl.ds(behind, QUARTER), :],
                pair_in.at[pack, 1],
                slot_sems.at[:, pack, 1],
                {"mode": left},
            ),
        ]

    def second_pass(pack):
        return [
            send(
                pair_mid.at[pack, 0],
                pair_sum.at[pack, 0],
                slot_sems.at[:, pack, 2],
                {"mode": right},
            ),
            send(
                pair_mid.at[pack, 1],
                pair_sum.at[pack, 1],
                slot_sems.at[:, pack, 3],
                {"mode": left},
            ),
        ]

    def in_place(pack, start, count, kind, peer):
        ref = factor.at[slots_of(pack), pl.ds(start, count), :]
        return send(ref, ref, slot_sems.at[:, pack, kind], {"mode": peer})

    def third_pass(pack, start_right=own_rows, start_left=own_rows):
        return [
            in_place(pack, start_right, QUARTER, 4, right),
            in_place(pack, start_left, QUARTER, 5, left),
        ]

    def fourth_pass(pack, top=left_rows, bottom=right_rows):
        return [
            in_place(pack, top, HALF, 6, right),
            in_place(pack, pl.multiple_of(bottom + HALF, 8), HALF, 7, left),
        ]

    def exit_wave(slot):
        for plane in range(2):
            patches[slot, plane] = take(slot, plane)
        probe_re, probe_im = probes[slot, 0], probes[slot, 1]
        patch_re, patch_im = patches[slot, 0], patches[slot, 1]
        return jnp.concatenate(
            [
                probe_re * patch_re - probe_im * patch_im,
                probe_re * patch_im + probe_im * patch_re,
            ],
            axis=1,
        )

    def forward(pack):
        slots = [pack * PACK + inner for inner in range(PACK)]
        wide = jnp.concatenate([exit_wave(slot) for slot in slots], axis=0)
        waves_out = both_sides(wide, table[0], table[1], table[2], table[3])
        for inner, slot in enumerate(slots):
            wave = waves_out[:, inner * SIDE : (inner + 1) * SIDE]
            far[slot] = wave
            strength = wave[:SIDE] * wave[:SIDE] + wave[SIDE:] * wave[SIDE:]
            power[slot, pl.ds(0, SIDE), :] = strength
            power[slot, pl.ds(SIDE, HALF), :] = strength[:HALF]

    def send_power(pack):
        forward(pack)
        for copy in first_pass(pack):
            copy.start()

    def relay_power(pack):
        slots = slots_of(pack)
        to_right, to_left = first_pass(pack)
        go_right, go_left = second_pass(pack)
        to_right.wait_recv()
        pair_mid[pack, 0] = (
            pair_in[pack, 0, :, pl.ds(HALF, HALF), :] + power[slots, pl.ds(right_rows, HALF), :]
        )
        go_right.start()
        to_left.wait_recv()
        pair_mid[pack, 1] = (
            pair_in[pack, 1, :, pl.ds(0, HALF), :]
            + power[slots, pl.ds(pl.multiple_of(left_rows + HALF, 8), HALF), :]
        )
        go_left.start()

    def make_factor(pack):
        for copy in second_pass(pack):
            copy.wait_recv()
        for inner in range(PACK):
            slot = pack * PACK + inner
            own = power[slot, pl.ds(own_rows, QUARTER), :]
            top = own[:HALF] + pair_sum[pack, 0, inner] + pair_in[pack, 1, inner, pl.ds(HALF, HALF), :]
            bottom = own[HALF:] + pair_sum[pack, 1, inner] + pair_in[pack, 0, inner, pl.ds(0, HALF), :]
            intensity = jnp.concatenate([top, bottom], axis=0)
            ratio = 1.0 - amps[slot] * lax.rsqrt(jnp.maximum(intensity, 1.0))
            factor[slot, pl.ds(own_rows, QUARTER), :] = jnp.where(slot < counts[0], ratio, 0.0)
        for copy in third_pass(pack):
            copy.start()

    def relay_factor(pack):
        from_left, from_right = third_pass(pack, left_rows, right_rows)
        go_right, go_left = fourth_pass(pack)
        from_left.wait_recv()
        go_right.start()
        from_right.wait_recv()
        go_left.start()

    def residue(slot):
        scale = factor[slot]
        wave = far[slot]
        return jnp.concatenate([wave[:SIDE] * scale, wave[SIDE:] * scale], axis=1)

    def backward(pack):
        slots = [pack * PACK + inner for inner in range(PACK)]
        wide = jnp.concatenate([residue(slot) for slot in slots], axis=0)
        backs = both_sides(wide, table[2], table[3], table[0], table[1])
        for inner, slot in enumerate(slots):
            add_gradients(slot, backs[:, inner * SIDE : (inner + 1) * SIDE])

    def add_gradients(slot, back):
        back_re, back_im = back[:SIDE], back[SIDE:]
        probe_re, probe_im = probes[slot, 0], probes[slot, 1]
        shift = place_of(slot)[2]
        grads = (
            probe_re * back_re + probe_im * back_im,
            probe_re * back_im - probe_im * back_re,
        )
        for plane in range(2):
            turned = pltpu.roll(grads[plane], shift & (SIDE - 1), 1)
            placed[plane, 2 * slot, pl.ds(SIDE, SIDE), :] = jnp.where(lane >= shift, turned, 0.0)
            placed[plane, 2 * slot + 1, pl.ds(SIDE, SIDE), :] = jnp.where(lane < shift, turned, 0.0)
        patch_re, patch_im = patches[slot, 0], patches[slot, 1]
        pieces = (
            patch_re * back_re + patch_im * back_im,
            patch_re * back_im - patch_im * back_re,
        )
        for at in range(COMP):
            for plane in range(2):
                where_at = pl.ds((2 * at + plane) * SIDE, SIDE)
                terms[where_at, :] = terms[where_at, :] + weights[at, slot] * pieces[plane]

    def use_factor(pack):
        facing = pl.multiple_of(QUARTER * lax.rem(mode + 2, MODES), 8)
        for copy in fourth_pass(pack, facing, facing):
            copy.wait_recv()
        backward(pack)

    stages = (send_power, relay_power, make_factor, relay_factor, use_factor)

    def step(at, carry):
        for place, stage in enumerate(stages):
            lag = LAGS[place]

            @pl.when((at >= lag) & (at < PACKS + lag))
            def _():
                stage(at - lag)

        return carry

    lax.fori_loop(0, PACKS + LAGS[-1], step, 0)

    def gathered(plane, tile_at, start):
        total = None
        for slot in range(SLOTS):
            row, base, shift = place_of(slot)
            index = jnp.where(
                tile_at == base, 2 * slot, jnp.where(tile_at == base + 1, 2 * slot + 1, EMPTY)
            )
            value = placed[plane, index, pl.ds(start - row, SIDE), :]
            total = value if total is None else total + value
        return total

    order = ((2, 0), (2, 1), (1, 1), (3, 0), (1, 0), (3, 1), (0, 0), (0, 1))

    def block_of(at):
        turn, plane = order[at]
        return lax.rem(mode + turn, MODES), plane

    def chunk_rows(at):
        return pl.ds(pl.multiple_of(at * rows, 8), rows)

    def half_of(ref, at):
        return ref.at[pl.ds(pl.multiple_of(at * half_rows, 8), half_rows)]

    halves = send(half_of(terms, 1 - core), half_in, pair_sems.at[:, 0], {"tile": sibling})
    halves.start()

    rims = []

    def send_rims(start, stop):
        for at in range(start, stop):
            block, plane = block_of(at)
            for half in range(2):
                rim_out[at, half] = gathered(plane, 2 * block + half, 2 * SIDE)
                copy = send(
                    rim_out.at[at, half],
                    rim_in.at[at, half],
                    rim_sems.at[:, at, half],
                    {"tile": below},
                )
                copy.start()
                rims.append(copy)

    send_rims(0, 2)
    halves.wait_recv()
    half_sum[...] = terms[pl.ds(pl.multiple_of(core * half_rows, 8), half_rows), :] + half_in[...]
    spread = []
    for step in range(1, across):
        copy = send(
            half_sum.at[chunk_rows(lax.rem(chip + step, across))],
            near_buf.at[step],
            near_sems.at[:, step],
            {"tile": near(step)},
        )
        copy.start()
        spread.append(copy)
    send_rims(2, 8)

    part_peers = ({"mode": right}, {"mode": left})
    part_kind = (0, 2, 1, 3, 4, 5)
    part_side = (0, 1, 0, 1, 0, 1)
    parts = [
        send(
            part.at[at, half],
            part_in.at[part_kind[at], half],
            part_sems.at[:, part_kind[at], half],
            part_peers[part_side[at]],
        )
        for at in range(6)
        for half in range(2)
    ]
    arrivals = {part_kind[at]: parts[2 * at : 2 * at + 2] for at in range(6)}

    def whole(at, extra):
        block, plane = block_of(at)
        for half in range(2):
            rims[2 * at + half].wait_recv()
            for kind in extra:
                arrivals[kind][half].wait_recv()
            value = gathered(plane, 2 * block + half, SIDE)
            value = value + jnp.where(tile > 0, rim_in[at, half], 0.0)
            for kind in extra:
                value = value + part_in[kind, half]
            yield half, value

    def to_owner(step):
        target = lax.rem(level + step, depth)
        at = pl.ds(pl.multiple_of(lax.rem(target, owners) * piece, 8), piece)
        return target, send(
            chunk.at[at], far_buf.at[step], far_sems.at[:, step], {"tile": beyond(step)}
        )

    def from_owner(source, step):
        at = pl.ds(pl.multiple_of(place * rows + lax.rem(source, owners) * piece, 8), piece)
        return send(
            probe_out.at[at], probe_out.at[at], back_sems.at[:, step], {"tile": beyond(step)}
        )

    for copy in spread:
        copy.wait_recv()
    total = half_sum[chunk_rows(chip), :]
    for step in range(1, across):
        total = total + near_buf[step]
    chunk[...] = total

    for step in range(1, depth):
        target, copy = to_owner(step)

        @pl.when(target < owners)
        def _():
            copy.start()

    for at in range(0, 4):
        for half, value in whole(at, ()):
            part[at, half] = value
            parts[2 * at + half].start()

    @pl.when(level < owners)
    def _():
        for step in range(1, depth):
            to_owner(step)[1].wait_recv()
        total = chunk[pl.ds(pl.multiple_of(lax.rem(level, owners) * piece, 8), piece), :]
        for step in range(1, depth):
            total = total + far_buf[step]
        at = pl.ds(pl.multiple_of(place * rows + lax.rem(level, owners) * piece, 8), piece)
        probe_out[at, :] = total
        for step in range(1, depth):
            from_owner(level, step).start()

    for at in range(4, 6):
        for half, value in whole(at, (2 * (at - 4),)):
            part[at, half] = value
            parts[2 * at + half].start()

    for step in range(1, depth):
        source = lax.rem(level - step + depth, depth)

        @pl.when(source < owners)
        def _():
            from_owner(source, step).wait_recv()

    def shared(source, step):
        at = chunk_rows(source)
        return send(
            probe_out.at[at], probe_out.at[at], spread_sems.at[:, step], {"tile": near(step)}
        )

    for step in range(1, across):
        shared(place, step).start()

    for step in range(1, across):
        shared(core * across + lax.rem(chip - step + across, across), step).wait_recv()

    def final(at):
        ref = half_of(probe_out, at)
        return send(ref, ref, pair_sems.at[:, 1], {"tile": sibling})

    final(core).start()
    for at in range(6, 8):
        for half, value in whole(at, (4, 3) if at == 6 else (5, 1)):
            object_out[at - 6, :, pl.ds(half * SIDE, SIDE)] = value
    final(1 - core).wait_recv()
    final(core).wait_send()
    halves.wait_send()
    for copy in halo + rims + parts + spread:
        copy.wait_send()
    for step in range(1, across):
        shared(place, step).wait_send()
    for step in range(1, depth):
        target, copy = to_owner(step)

        @pl.when(target < owners)
        def _():
            copy.wait_send()

    @pl.when(level < owners)
    def _():
        for step in range(1, depth):
            from_owner(level, step).wait_send()

    def settle(pack, carry):
        for make in (first_pass, second_pass, third_pass, fourth_pass):
            for copy in make(pack):
                copy.wait_send()
        return carry

    lax.fori_loop(0, PACKS, settle, 0)


def tables():
    line = np.arange(SIDE)
    angle = (line[:, None] * line[None, :] % SIDE) * (2.0 * math.pi / SIDE)
    cos = np.cos(angle) / math.sqrt(SIDE)
    sin = -np.sin(angle) / math.sqrt(SIDE)
    return np.stack([cos, sin]).astype(np.float32)


def local(object_field, components, relax_weights, amplitudes, positions, counts):
    tiles = lax.axis_size("tile")
    group = group_size(tiles)
    depth = tiles // group
    rows = COMP * 2 * SIDE // group
    piece = rows // owner_count(depth)
    f32 = jnp.float32
    anywhere = pl.BlockSpec(memory_space=pltpu.HBM)
    vector = pl.BlockSpec(memory_space=pltpu.VMEM)
    flops = 2 * 2 * SLOTS * 3 * 2 * 256 * 256 * 128
    object_grad, probe_grad = pl.pallas_call(
        functools.partial(kernel, tiles),
        out_shape=(
            jax.ShapeDtypeStruct((2, SIDE, 2 * SIDE), f32),
            jax.ShapeDtypeStruct((COMP * 2 * SIDE, SIDE), f32),
        ),
        in_specs=[anywhere] * 7,
        out_specs=(vector, vector),
        scratch_shapes=[
            pltpu.SMEM((COMP, SLOTS), f32),
            pltpu.SMEM((2, SLOTS), jnp.int32),
            pltpu.SMEM((1,), jnp.int32),
            pltpu.VMEM((4, 2 * SIDE, 2 * SIDE), jnp.bfloat16),
            pltpu.VMEM((2, SIDE, SIDE), f32),
            pltpu.VMEM((2, TILES_WIDE, 2 * SIDE, SIDE), f32),
            pltpu.VMEM((COMP, 2, SIDE, SIDE), f32),
            pltpu.VMEM((SLOTS, QUARTER, SIDE), f32),
            pltpu.VMEM((SLOTS, 2, SIDE, SIDE), f32),
            pltpu.VMEM((SLOTS, 2, SIDE, SIDE), f32),
            pltpu.VMEM((SLOTS, 2 * SIDE, SIDE), f32),
            pltpu.VMEM((SLOTS, SIDE + HALF, SIDE), f32),
            pltpu.VMEM((PACKS, 2, PACK, QUARTER, SIDE), f32),
            pltpu.VMEM((PACKS, 2, PACK, HALF, SIDE), f32),
            pltpu.VMEM((PACKS, 2, PACK, HALF, SIDE), f32),
            pltpu.VMEM((SLOTS, SIDE, SIDE), f32),
            pltpu.VMEM((2, EMPTY + 1, 3 * SIDE, SIDE), f32),
            pltpu.VMEM((8, 2, SIDE, SIDE), f32),
            pltpu.VMEM((8, 2, SIDE, SIDE), f32),
            pltpu.VMEM((6, 2, SIDE, SIDE), f32),
            pltpu.VMEM((6, 2, SIDE, SIDE), f32),
            pltpu.VMEM((COMP * 2 * SIDE, SIDE), f32),
            pltpu.VMEM((COMP * SIDE, SIDE), f32),
            pltpu.VMEM((COMP * SIDE, SIDE), f32),
            pltpu.VMEM((rows, SIDE), f32),
            pltpu.VMEM((group // 2, rows, SIDE), f32),
            pltpu.VMEM((depth, piece, SIDE), f32),
            pltpu.SemaphoreType.DMA((6 + TILES_WIDE,)),
            pltpu.SemaphoreType.DMA((2, TILES_WIDE)),
            pltpu.SemaphoreType.DMA((2, PACKS, 8)),
            pltpu.SemaphoreType.DMA((2, 8, 2)),
            pltpu.SemaphoreType.DMA((2, 6, 2)),
            pltpu.SemaphoreType.DMA((2, 2)),
            pltpu.SemaphoreType.DMA((2, group // 2)),
            pltpu.SemaphoreType.DMA((2, depth)),
            pltpu.SemaphoreType.DMA((2, depth)),
            pltpu.SemaphoreType.DMA((2, group // 2)),
        ],
        compiler_params=pltpu.CompilerParams(
            collective_id=0, has_side_effects=True, vmem_limit_bytes=62 * 1024 * 1024
        ),
        cost_estimate=pl.CostEstimate(
            flops=flops, bytes_accessed=4 * 1024 * 1024, transcendentals=SLOTS * SIDE * SIDE
        ),
    )(
        object_field,
        components,
        relax_weights.T,
        amplitudes,
        positions.T,
        counts,
        jnp.asarray(tables()),
    )
    return object_grad, probe_grad.reshape(1, COMP, 2, SIDE, SIDE)


def solution(mesh):
    return jax.shard_map(
        local,
        mesh=mesh,
        in_specs=(
            P(None, "tile", None),
            P("mode", None, None, None, None),
            P("tile", None),
            P("tile", None, None),
            P("tile", None),
            P("tile"),
        ),
        out_specs=(P(None, "tile", "mode"), P("mode", None, None, None, None)),
        check_vma=False,
    )
```
